128 devices in a mesh: tp: 4 (over z), pool: 32 (over y, x, core).
Axes of the slice: x: 4, y: 4, z: 4, core: 2. Of those that a mesh axis runs over, the one named last changes fastest.
Arguments:
- queries: bfloat16 [512, 4, 8192], P('pool', None, 'tp'), may hold values from -8 to 8
- home_keys: bfloat16 [512, 512, 1024], P('pool', None, 'tp'), may hold values from -6.5 to 6.5
- home_values: bfloat16 [512, 512, 1024], P('pool', None, 'tp'), may hold values from -4 to 4
- new_keys: bfloat16 [512, 4, 1024], P('pool', None, 'tp'), may hold values from -4 to 4
- new_values: bfloat16 [512, 4, 1024], P('pool', None, 'tp'), may hold values from -4 to 4
- home_len: int32 [512], P('pool'), may hold values from 2 to 512
- piece_keys: bfloat16 [512, 256, 1024], P('pool', None, 'tp'), may hold values from -4 to 4
- piece_values: bfloat16 [512, 256, 1024], P('pool', None, 'tp'), may hold values from -4 to 4
- lend_request: int32 [512], P('pool'), may hold values from 0 to 511, as said below
- lend_blocks: int32 [512], P('pool'), may hold values from 1 to 2
- out_weight: bfloat16 [8192, 4096], P('tp'), may hold values from -0.5 to 0.5
Outputs:
- projected: bfloat16 [512, 4, 4096], P('pool', None, 'tp')
The draws below stay inside these ranges and needn't reach their ends.
Inputs may be any that keep to these rules, and one draw needn't show every extreme that they name: `lend_request`: entries b * 16 to (b + 1) * 16 - 1 are the slots of pool index b. Request r is owned by pool index r // 16. Among the slots of one pool index at most 1 hold requests of the same owner, and some owner has exactly 1 slots on every pool index.
All inputs are finite; a program needn't handle non-finite values.
Results may differ from the reference program's by a relative error of at most 0.0055.
Values may be sent and summed in bfloat16 or wider, within the bound.
A program may use at most 128 MiB of HBM per device.

```python
import math
import jax
import jax.numpy as jnp
from jax import lax

QH = 64
KVH = 8
HD = 128
D_OUT = 4096
STEPS = 4
BLOCK = 128
PIECE_BLK = 2
R_DEV = 16
HOME = 512
LEND = 16
REQUESTS = 512
N_POOL = 32


def draw_queries(key, part):
    key = jax.random.fold_in(key, 11)
    base_key = jax.random.fold_in(key, 0)
    base = jax.random.truncated_normal(base_key, -4.0, 4.0, (REQUESTS, STEPS, QH, HD), jnp.float32)
    return base.reshape(REQUESTS, STEPS, QH * HD).astype(jnp.bfloat16)


def draw_home_keys(key, part):
    key = jax.random.fold_in(key, 17)
    base = jax.random.truncated_normal(key, -4.0, 4.0, (REQUESTS, HOME, KVH, HD), jnp.float32)
    return base.reshape(REQUESTS, HOME, KVH * HD).astype(jnp.bfloat16)


def draw_home_len(key, part):
    key = jax.random.fold_in(key, 23)
    len_key, pick_key = jax.random.split(key)
    lengths = jax.random.randint(len_key, (REQUESTS,), 2, HOME + 1)
    chosen = jax.random.randint(pick_key, (), 0, REQUESTS)
    return jnp.where(jnp.arange(REQUESTS, dtype=jnp.int32) == chosen, HOME, lengths).astype(jnp.int32)


def draw_lend_blocks(key, part):
    key = jax.random.fold_in(key, 29)
    len_key, pick_key = jax.random.split(key)
    total_slots = N_POOL * LEND
    blocks = jax.random.randint(len_key, (total_slots,), 1, PIECE_BLK + 1)
    chosen = jax.random.randint(pick_key, (), 0, total_slots)
    return jnp.where(jnp.arange(total_slots, dtype=jnp.int32) == chosen, PIECE_BLK, blocks).astype(jnp.int32)


def draw_lend_request(key, part):
    key = jax.random.fold_in(key, 31)
    capacity = max(1, 2 * LEND // N_POOL)
    busy_key, rest_key = jax.random.split(key)
    busiest = jax.random.randint(busy_key, (), 0, N_POOL)

    def lender(lender_key):
        order_key, pair_key, slot_key, local_key = jax.random.split(lender_key, 4)
        others = (busiest + 1 + jax.random.permutation(order_key, N_POOL - 1)) % N_POOL
        pair_list = jax.random.permutation(pair_key, jnp.repeat(others, capacity))[:LEND - capacity]
        owners = jnp.concatenate([jnp.full((capacity,), busiest, jnp.int32), pair_list.astype(jnp.int32)])
        owners = jax.random.permutation(slot_key, owners)
        local_row = jax.random.randint(local_key, (LEND,), 0, R_DEV)
        return (owners * R_DEV + local_row).astype(jnp.int32)
    return jax.vmap(lender)(jax.random.split(rest_key, N_POOL)).reshape(N_POOL * LEND)


def block_levels(rng, extent, shards, smallest, high):
    gain = 1.0
    for dim, blocks in shards:
        draws = jax.random.uniform(jax.random.fold_in(jax.random.fold_in(rng, 6), dim), (blocks,), jnp.float32, smallest / len(shards), high / len(shards))
        gain = gain * jnp.repeat(jnp.exp(draws), extent[dim] // blocks).reshape((-1,) + (1,) * (len(extent) - 1 - dim))
    return gain


def scatter_about(own_key, extent, spread, most, cuts=(), kind=jnp.bfloat16):
    result = jax.random.normal(own_key, extent, jnp.float32) * spread
    if len(cuts) > 0:
        result = block_levels(own_key, extent, cuts, -0.22, 0.18) * result
    return jnp.clip(result, min=-most, max=most).astype(kind)


def setup_inputs(seed: int = 0) -> dict:
    key_list = jax.random.split(jax.random.key(seed), 12)
    queries = draw_queries(jax.random.fold_in(key_list[11], 71), 0)
    home_keys = draw_home_keys(jax.random.fold_in(key_list[11], 71), 0)
    home_values = scatter_about(key_list[2], (REQUESTS, HOME, KVH * HD), 1.0, 4.0, ((0, 32), (2, 4)))
    new_keys = scatter_about(key_list[3], (REQUESTS, STEPS, KVH * HD), 1.0, 4.0, ((0, 32), (2, 4)))
    new_values = scatter_about(key_list[4], (REQUESTS, STEPS, KVH * HD), 1.0, 4.0, ((0, 32), (2, 4)))
    home_len = draw_home_len(jax.random.fold_in(key_list[11], 71), 0)
    piece_keys = scatter_about(key_list[6], (N_POOL * LEND, PIECE_BLK * BLOCK, KVH * HD), 1.0, 4.0, ((0, 32), (2, 4)))
    piece_values = scatter_about(key_list[7], (N_POOL * LEND, PIECE_BLK * BLOCK, KVH * HD), 1.0, 4.0, ((0, 32), (2, 4)))
    lend_request = draw_lend_request(jax.random.fold_in(key_list[11], 71), 0)
    lend_blocks = draw_lend_blocks(jax.random.fold_in(key_list[11], 71), 0)
    out_weight = scatter_about(key_list[10], (QH * HD, D_OUT), (QH * HD // 64) ** -0.5, 0.5, ((0, 4),))
    return dict(queries=queries, home_keys=home_keys, home_values=home_values, new_keys=new_keys, new_values=new_values, home_len=home_len, piece_keys=piece_keys, piece_values=piece_values, lend_request=lend_request, lend_blocks=lend_blocks, out_weight=out_weight)


MASKED_SCORE = -1e+30

def rounded(values):
    return lax.optimization_barrier(values.astype(jnp.bfloat16)).astype(jnp.float32)

def part_summary(score_sets, value_sets, patterns):
    highest = lax.optimization_barrier(jnp.max(score_sets[0], axis=-1))
    for scores in score_sets[1:]:
        highest = jnp.maximum(highest, lax.optimization_barrier(jnp.max(scores, axis=-1)))
    summed = jnp.zeros(highest.shape, jnp.float32)
    weighted = None
    for scores, values, pattern in zip(score_sets, value_sets, patterns):
        shares = jnp.exp(scores - highest[..., None])
        summed = summed + lax.optimization_barrier(jnp.sum(shares, axis=-1))
        addend = jnp.einsum(pattern, rounded(shares), values)
        weighted = addend if weighted is None else weighted + addend
    return (highest + jnp.log(summed), weighted / summed[..., None])

def reference(queries, home_keys, home_values, new_keys, new_values, home_len, piece_keys, piece_values, lend_request, lend_blocks, out_weight):
    per_group = QH // KVH
    scaling = 1.0 / math.sqrt(HD)
    query_rows = queries.astype(jnp.float32).reshape(REQUESTS, STEPS, KVH, per_group, HD)
    keys_home = home_keys.astype(jnp.float32).reshape(REQUESTS, HOME, KVH, HD)
    values_home = home_values.astype(jnp.float32).reshape(REQUESTS, HOME, KVH, HD)
    keys_new = new_keys.astype(jnp.float32).reshape(REQUESTS, STEPS, KVH, HD)
    values_new = new_values.astype(jnp.float32).reshape(REQUESTS, STEPS, KVH, HD)
    home_scores = jnp.einsum('rsgha,rtga->rghst', query_rows, keys_home) * scaling
    home_valid = jnp.arange(HOME, dtype=jnp.int32)[None, :] < home_len[:, None]
    home_scores = jnp.where(home_valid[:, None, None, None, :], home_scores, MASKED_SCORE)
    new_scores = jnp.einsum('rsgha,ruga->rghsu', query_rows, keys_new) * scaling
    causal = jnp.arange(STEPS, dtype=jnp.int32)[None, :] <= jnp.arange(STEPS, dtype=jnp.int32)[:, None]
    new_scores = jnp.where(causal, new_scores, MASKED_SCORE)
    home_lse, home_out = part_summary([home_scores, new_scores], [values_home, values_new], ['rghst,rtga->rghsa', 'rghsu,ruga->rghsa'])
    slot_count = N_POOL * LEND
    piece_len = PIECE_BLK * BLOCK
    slot_query = query_rows[lend_request]
    keys_piece = piece_keys.astype(jnp.float32).reshape(slot_count, piece_len, KVH, HD)
    values_piece = piece_values.astype(jnp.float32).reshape(slot_count, piece_len, KVH, HD)
    piece_scores = jnp.einsum('lsgha,ltga->lghst', slot_query, keys_piece) * scaling
    piece_valid = jnp.arange(piece_len, dtype=jnp.int32)[None, :] < (lend_blocks * BLOCK)[:, None]
    piece_scores = jnp.where(piece_valid[:, None, None, None, :], piece_scores, MASKED_SCORE)
    piece_lse, piece_out = part_summary([piece_scores], [values_piece], ['lghst,ltga->lghsa'])
    member = lend_request[None, :] == jnp.arange(REQUESTS, dtype=jnp.int32)[:, None]
    piece_top = lax.optimization_barrier(jnp.max(jnp.where(member[:, :, None, None, None], piece_lse[None], MASKED_SCORE), axis=1))
    highest = jnp.maximum(home_lse, piece_top)
    piece_weight = jnp.exp(piece_lse - highest[lend_request])
    numerator = jax.ops.segment_sum(piece_weight[..., None] * piece_out, lend_request, num_segments=REQUESTS)
    denominator = jax.ops.segment_sum(piece_weight, lend_request, num_segments=REQUESTS)
    home_weight = jnp.exp(home_lse - highest)
    numerator = numerator + home_weight[..., None] * home_out
    denominator = denominator + home_weight
    attention = (numerator / denominator[..., None]).transpose(0, 3, 1, 2, 4).reshape(REQUESTS * STEPS, QH * HD).astype(jnp.bfloat16)
    projected = jnp.dot(attention, out_weight, preferred_element_type=jnp.float32)
    return projected.astype(jnp.bfloat16).reshape(REQUESTS, STEPS, D_OUT)
```

```python
import functools
import math

import jax
import jax.numpy as jnp
from jax import lax
from jax.experimental import pallas as pl
from jax.experimental.pallas import tpu as pltpu
from jax.sharding import PartitionSpec as P

QH = 64
KVH = 8
HD = 128
BLOCK = 128
MASKED = -1e30
MESH = pl.DeviceIdType.MESH
F32 = jnp.float32
BF16 = jnp.bfloat16
COEF = math.log2(math.e) / math.sqrt(HD)


def nt(a, b):
    return lax.dot_general(a, b, (((1,), (1,)), ((), ())), preferred_element_type=F32)


def nn(a, b):
    return lax.dot_general(a, b, (((1,), (0,)), ((), ())), preferred_element_type=F32)


def iota(shape, dim):
    return lax.broadcasted_iota(jnp.int32, shape, dim)


def attend(q, keys, values, valid_len, new_scores, new_values):
    half = q.shape[0] // 2
    zero = jnp.zeros((half, HD), BF16)
    wide = jnp.concatenate(
        [
            jnp.concatenate([q[:half], zero], axis=1),
            jnp.concatenate([zero, q[half:]], axis=1),
        ],
        axis=0,
    )
    scores = nt(wide, keys)
    scores = jnp.where(iota(scores.shape, 1) < valid_len, scores, MASKED)
    top = jnp.max(scores, axis=1, keepdims=True)
    top = jnp.maximum(top, jnp.max(new_scores, axis=1, keepdims=True))
    shares = jnp.exp2((scores - top) * COEF)
    summed = jnp.sum(shares, axis=1, keepdims=True)
    both = nn(shares.astype(BF16), values)
    out = jnp.concatenate([both[:half, :HD], both[half:, HD:]], axis=0)
    new_shares = jnp.exp2((new_scores - top) * COEF)
    summed = summed + jnp.sum(new_shares, axis=1, keepdims=True)
    out = out + nn(new_shares.astype(BF16), new_values)
    return (out / summed).astype(BF16), top * COEF + jnp.log2(summed)


def head_shares(q, keys, valid_len):
    scores = nt(q, keys)
    scores = jnp.where(iota(scores.shape, 1) < valid_len, scores, MASKED)
    top = jnp.max(scores, axis=1, keepdims=True)
    shares = jnp.exp2((scores - top) * COEF)
    summed = jnp.sum(shares, axis=1, keepdims=True)
    return shares.astype(BF16), summed, top * COEF + jnp.log2(summed)


def kernel(
    n, t,
    hlen_h, lreq_h, lblk_h, q_h, nk_h, nv_h, hk_h, hv_h, pk_h, pv_h, w_h,
    out_ref,
    hlen, lreq, lblk, q_v, nk_v, nv_v, hk_v, hv_v, pk_v, pv_v, w_v,
    sn_v, tab_s, tab_r, inv_v, inv_s,
    qs0_v, qs1_v, qr0_v, qr1_v, res_v, sh_v, rs0_v, rs1_v, rr0_v, rr1_v, ls_v, lr_v,
    ho_v, hl_c, pl_c, e_v, t_v, a0_v, a1_v, acc_v, ps_v, pr_v,
    in_sem, home_sem, w_sem, send_sem, recv_sem, rsend_sem, rrecv_sem,
):
    me = lax.axis_index("pool")
    tp = lax.axis_index("tp")
    reqs, rows, _ = q_v.shape
    slots = pk_v.shape[0]
    steps = 4
    home_chunks = home_sem.shape[1]
    per_chunk = reqs // home_chunks
    cols = w_v.shape[2]
    part_rows = rows // 2
    deep = a0_v.shape[1]
    qs, qr = (qs0_v, qs1_v), (qr0_v, qr1_v)
    rs, rr = (rs0_v, rs1_v), (rr0_v, rr1_v)

    def pool_peer(d):
        return jnp.where(me + d >= n, me + d - n, me + d)

    def tp_peer(d):
        return lax.rem(tp + d, t)

    barrier = pltpu.get_barrier_semaphore()

    for d in range(1, n):
        pl.semaphore_signal(
            barrier, inc=1, device_id={"pool": pool_peer(d)}, device_id_type=MESH
        )
    for d in range(1, t):
        pl.semaphore_signal(
            barrier, inc=1, device_id={"tp": tp_peer(d)}, device_id_type=MESH
        )

    small = [
        pltpu.make_async_copy(src, dst, in_sem.at[i])
        for i, (src, dst) in enumerate(
            [
                (q_h, q_v), (nk_h, nk_v), (nv_h, nv_v), (pk_h, pk_v), (pv_h, pv_v),
                (lreq_h, lreq), (hlen_h, hlen), (lblk_h, lblk),
            ]
        )
    ]
    for i in (5, 6, 7, 0, 1, 2):
        small[i].start()
    home = []
    for c in range(home_chunks):
        part = pl.ds(c * per_chunk, per_chunk)
        home.append(
            [
                pltpu.make_async_copy(hk_h.at[part], hk_v.at[part], home_sem.at[0, c]),
                pltpu.make_async_copy(hv_h.at[part], hv_v.at[part], home_sem.at[1, c]),
            ]
        )
    order = [2, 1, 3, 0]
    weights = []
    for i, d in enumerate(order):
        column = pl.multiple_of(tp_peer(d) * cols, cols)
        weights.append(
            pltpu.make_async_copy(w_h.at[:, pl.ds(column, cols)], w_v.at[i], w_sem.at[i])
        )

    for i in (5, 6, 7):
        small[i].wait()
    owner_id = iota((n, 128), 0)
    wanted = jnp.full((n, 128), -1, jnp.int32)
    slot_of = jnp.zeros((n, 128), jnp.int32)
    for l in range(slots):
        request = lreq[l]
        owner = request // reqs
        hit = owner_id == owner
        wanted = jnp.where(hit, request - owner * reqs, wanted)
        slot_of = jnp.where(hit, l, slot_of)
    tab_s[...] = wanted.reshape(n, 1, 128)
    inv_v[...] = slot_of.reshape(n, 1, 128)

    def remote(phase, src, dst, d):
        return pltpu.make_async_remote_copy(
            src_ref=src,
            dst_ref=dst,
            send_sem=send_sem.at[phase],
            recv_sem=recv_sem.at[phase],
            device_id={"pool": pool_peer(d)},
            device_id_type=MESH,
        )

    def all_of(phase, buffer):
        part = buffer.at[pl.ds(0, n - 1)]
        return remote(phase, part, part, 1)

    pl.semaphore_wait(barrier, n - 1 + t - 1)

    for d in range(1, n):
        remote(0, tab_s.at[pool_peer(d)], tab_r.at[me], d).start()
    tab_r[me] = tab_s[me]
    for c in range(home_chunks):
        home[c][0].start()
        home[c][1].start()
    small[3].start()
    small[4].start()

    for copy in small[:3]:
        copy.wait()
    sn_v[...] = nt(q_v[...].reshape(reqs * rows, HD), nk_v[...]).reshape(reqs, rows, HD)
    hl_c[...] = jnp.zeros(hl_c.shape, F32)
    pl_c[...] = jnp.zeros(pl_c.shape, F32)
    lane = iota((rows, 128), 1)
    row = iota((rows, 128), 0)

    def home_request(r):
        low = r * (2 * steps) + (row // (rows // 2)) * steps
        seen = (lane >= low) & (lane <= low + row % steps)
        new_scores = jnp.where(seen, sn_v[r], MASKED)
        out, lse = attend(q_v[r], hk_v[r], hv_v[r], hlen[r], new_scores, nv_v[...])
        ho_v[r] = out
        return lse

    def home_pair(i, carry):
        lse0 = home_request(2 * i)
        lse1 = home_request(2 * i + 1)
        hl_c[0:rows] = jnp.where(
            lane == 2 * i, lse0, jnp.where(lane == 2 * i + 1, lse1, hl_c[0:rows])
        )
        return carry

    def home_part(c):
        home[c][0].wait()
        home[c][1].wait()
        lax.fori_loop(c * per_chunk // 2, (c + 1) * per_chunk // 2, home_pair, 0)

    home_part(0)

    all_of(0, tab_r).wait_recv()

    picks = [jnp.maximum(tab_r[pool_peer(d), 0, 0], 0) for d in range(1, n)]
    mine = jnp.maximum(tab_r[me, 0, 0], 0)
    halves = [slice(0, part_rows), slice(part_rows, rows)]

    def send_query(k, d):
        peer = pool_peer(d)
        qs[k][peer] = q_v[picks[d - 1], halves[k]]
        remote(1 + k, qs[k].at[peer], qr[k].at[me], d).start()

    for k in range(2):
        qr[k][me] = q_v[mine, halves[k]]
    for d in range(1, n):
        send_query(0, d)
    for copy in weights:
        copy.start()

    home[1][0].wait()
    home[1][1].wait()
    for i in range(per_chunk // 2):
        for d in range(1 + i * 16, min(n, 17 + i * 16)):
            send_query(1, d)
        home_pair(per_chunk // 2 + i, 0)
    for d in range(n):
        inv_s[d] = inv_v[pool_peer(d), 0, 0]

    small[3].wait()
    small[4].wait()
    part_lane = iota((part_rows, 128), 1)

    def send_result(k, d):
        peer = pool_peer(d)
        rs[k][peer] = res_v[inv_s[d], halves[k]]
        remote(4 + k, rs[k].at[peer], rr[k].at[me], d).start()

    def send_lse(d):
        remote(3, ls_v.at[pool_peer(d)], lr_v.at[me], d).start()

    for k in range(2):
        all_of(1 + k, qr[k]).wait_recv()
        width = slice(k * HD, k * HD + HD)
        total = jnp.zeros((part_rows, 128), F32)
        sums = []
        for l in range(slots):
            owner = lreq[l] // reqs
            shares, summed, lse = head_shares(qr[k][owner], pk_v[l, :, width], lblk[l] * BLOCK)
            sh_v[l] = shares
            sums.append(summed)
            total = jnp.where(part_lane == owner, lse, total)
            if k == 1:
                for d in (2 * l, 2 * l + 1):
                    if d > 0:
                        send_result(0, d)
        pl_c[halves[k]] = total
        if k == 1:
            ls_v[...] = pl_c[...].T[0:n].reshape(n, 1, 128)
            lr_v[me] = ls_v[me]
        for l in range(slots):
            out = nn(sh_v[l], pv_v[l, :, width])
            res_v[l, halves[k]] = (out / sums[l]).astype(BF16)
            if k == 1:
                for d in (2 * l, 2 * l + 1):
                    if d > 0:
                        send_lse(d)
        rr[k][me] = res_v[inv_s[0], halves[k]]
    for d in range(1, n):
        send_result(1, d)

    for c in range(2, home_chunks):
        home_part(c)

    eight = iota((8, 128), 1) // 16 == iota((8, 128), 0)
    local = tab_r[...].reshape(n, 128)
    parts = n + reqs
    seg = jnp.concatenate([local, iota((reqs, 128), 0)], axis=0)
    seg_lane = jnp.concatenate(
        [
            jnp.sum(jnp.where(eight, seg[c * 8 : c * 8 + 8], 0), axis=0, keepdims=True)
            for c in range(parts // 8)
        ],
        axis=1,
    )
    block = (16, parts * 16)
    b_row, b_col = iota(block, 0), iota(block, 1)
    head_step = b_col % 16 - b_row % steps
    owner_row = seg_lane - b_row // steps
    for i in range(16):
        same = (head_step == i // 4 * steps) & (owner_row == i % 4 * 4)
        e_v[i] = jnp.where(same, 1.0, 0.0).astype(BF16)
    t_row = iota(t_v.shape, 0)
    t_col = iota(t_v.shape, 1)
    t_v[...] = jnp.where(
        t_row == (t_col // 128) * 16 + t_col % 16, 1.0, 0.0
    ).astype(BF16)

    all_of(3, lr_v).wait_recv()
    lse = jnp.concatenate([lr_v[...].reshape(n, 128), hl_c[...].T[0:reqs]], axis=0)
    big = lse
    for r in range(reqs):
        hit = seg == r
        big = jnp.where(hit, jnp.max(jnp.where(hit, lse, MASKED), axis=0, keepdims=True), big)
    share = jnp.where(seg >= 0, jnp.exp2(lse - big), 0.0)
    total = jnp.ones_like(share)
    for r in range(reqs):
        hit = seg == r
        total = jnp.where(
            hit, jnp.sum(jnp.where(hit, share, 0.0), axis=0, keepdims=True), total
        )
    spread = nn((share / total).astype(BF16), t_v[...])

    def merge(k, a_v):
        all_of(4 + k, rr[k]).wait_recv()
        for g in range(part_rows // 16):
            wide = (k * (part_rows // 16) + g) * 128
            along = jnp.concatenate(
                [
                    jnp.sum(
                        jnp.where(
                            eight, spread[c * 8 : c * 8 + 8, wide : wide + 128], 0.0
                        ),
                        axis=0,
                        keepdims=True,
                    )
                    for c in range(parts // 8)
                ],
                axis=1,
            )
            along = jnp.broadcast_to(along, block).astype(BF16)
            left = (e_v[...] * along[None]).reshape(256, parts * 16)
            group = slice(g * 16, g * 16 + 16)
            own = slice(k * part_rows + g * 16, k * part_rows + g * 16 + 16)
            right = jnp.concatenate(
                [rr[k][:, group].reshape(n * 16, HD), ho_v[:, own].reshape(reqs * 16, HD)],
                axis=0,
            )
            merged = nn(left, right).astype(BF16)
            for h in range(4):
                head = g * 4 + h
                a_v[:, head * HD : head * HD + HD] = merged[h * rows : h * rows + rows]

    merge(0, a0_v)
    for i in range(t):
        weights[i].wait()
        acc_v[i] = nn(a0_v[...], w_v[i, 0:deep])
    merge(1, a1_v)

    def projected(i):
        return acc_v[i] + nn(a1_v[...], w_v[i, deep : 2 * deep])

    half = cols // 2

    def to_neighbour(i, src, side):
        return pltpu.make_async_remote_copy(
            src_ref=src,
            dst_ref=pr_v.at[i],
            send_sem=rsend_sem.at[i],
            recv_sem=rrecv_sem.at[i],
            device_id={"tp": tp_peer(side)},
            device_id_type=MESH,
        )

    up, down = 1, t - 1
    hops = [
        to_neighbour(i, ps_v.at[i], side)
        for i, side in enumerate([up, down, up, down, up, down])
    ]
    for i in range(2):
        at = slice(i * half, i * half + half)
        value = acc_v[0, :, at] + nn(a1_v[...], w_v[0, deep : 2 * deep, at])
        ps_v[i] = value.astype(BF16)
        hops[i].start()
    above = projected(1)
    ps_v[2] = above[:, half:].astype(BF16)
    hops[2].start()
    acc_v[1, :, :half] = above[:, :half]
    below = projected(2)
    ps_v[3] = below[:, :half].astype(BF16)
    hops[3].start()
    hops[0].wait_recv()
    ps_v[4] = (acc_v[1, :, :half] + pr_v[0].astype(F32)).astype(BF16)
    hops[4].start()
    hops[1].wait_recv()
    ps_v[5] = (below[:, half:] + pr_v[1].astype(F32)).astype(BF16)
    hops[5].start()
    acc_v[3] = projected(3)
    for i in range(2, 6):
        hops[i].wait_recv()
    from_below = jnp.concatenate([pr_v[4], pr_v[2]], axis=1).astype(F32)
    from_above = jnp.concatenate([pr_v[3], pr_v[5]], axis=1).astype(F32)
    result = acc_v[3] + from_below + from_above

    first = iota((8, 8, HD), 1) < 4
    for g in range(2):
        even, odd = [], []
        for k in range(2):
            c = (g * 2 + k) * 2 * HD
            left = result[:, c : c + HD].reshape(8, 8, HD)
            right = result[:, c + HD : c + 2 * HD].reshape(8, 8, HD)
            even.append(jnp.where(first, left, pltpu.roll(right, 4, 1)))
            odd.append(jnp.where(first, pltpu.roll(left, 4, 1), right))
        for k, both in enumerate([even, odd]):
            out_ref[:, k, g * 16 : g * 16 + 16] = jnp.concatenate(both, axis=1).astype(BF16)

    all_of(0, tab_s).wait_send()
    for k in range(2):
        all_of(1 + k, qs[k]).wait_send()
        all_of(4 + k, rs[k]).wait_send()
    all_of(3, ls_v).wait_send()
    for hop in hops:
        hop.wait_send()


def per_device(
    queries, home_keys, home_values, new_keys, new_values, home_len,
    piece_keys, piece_values, lend_request, lend_blocks, out_weight,
):
    n = lax.axis_size("pool")
    t = lax.axis_size("tp")
    reqs, steps, features = queries.shape
    heads = features // HD
    kv = new_keys.shape[2] // HD
    rows = heads * steps
    slots, piece = piece_keys.shape[:2]
    cols = out_weight.shape[1] // t

    def head_rows(x):
        count = x.shape[2] // HD
        return x.reshape(reqs, steps, count, HD).transpose(0, 2, 1, 3)

    q = head_rows(queries).reshape(reqs, rows, HD)
    nk = head_rows(new_keys).reshape(reqs * kv * steps, HD)
    nv = head_rows(new_values).reshape(reqs * kv * steps, HD)
    hbm = pl.BlockSpec(memory_space=pl.ANY)
    chunks = 4
    vmem = pltpu.VMEM
    out = pl.pallas_call(
        functools.partial(kernel, n, t),
        out_shape=vmem((reqs // 2, 2, cols // HD * steps, HD), BF16),
        in_specs=[hbm] * 11,
        out_specs=pl.BlockSpec(memory_space=pltpu.VMEM),
        scratch_shapes=[
            *[pltpu.SMEM((reqs,), jnp.int32)] * 3,
            vmem(q.shape, BF16),
            vmem(nk.shape, BF16),
            vmem(nv.shape, BF16),
            vmem(home_keys.shape, BF16),
            vmem(home_values.shape, BF16),
            vmem(piece_keys.shape, BF16),
            vmem(piece_values.shape, BF16),
            vmem((t, features, cols), BF16),
            vmem((reqs, rows, 128), F32),
            vmem((n, 1, 128), jnp.int32),
            vmem((n, 1, 128), jnp.int32),
            vmem((n, 1, 128), jnp.int32),
            pltpu.SMEM((n,), jnp.int32),
            *[vmem((n, rows // 2, HD), BF16)] * 4,
            vmem((slots, rows, HD), BF16),
            vmem((slots, rows // 2, piece), BF16),
            *[vmem((n, rows // 2, HD), BF16)] * 4,
            *[vmem((n, 1, 128), F32)] * 2,
            vmem((reqs, rows, HD), BF16),
            *[vmem((128, 128), F32)] * 2,
            vmem((16, 16, (n + reqs) * 16), BF16),
            vmem((128, (rows // 16) * 128), BF16),
            *[vmem((reqs * steps, features // 2), BF16)] * 2,
            vmem((t, reqs * steps, cols), F32),
            vmem((6, reqs * steps, cols // 2), BF16),
            vmem((6, reqs * steps, cols // 2), BF16),
            pltpu.SemaphoreType.DMA((8,)),
            pltpu.SemaphoreType.DMA((2, chunks)),
            pltpu.SemaphoreType.DMA((t,)),
            pltpu.SemaphoreType.DMA((6,)),
            pltpu.SemaphoreType.DMA((6,)),
            pltpu.SemaphoreType.DMA((6,)),
            pltpu.SemaphoreType.DMA((6,)),
        ],
        compiler_params=pltpu.CompilerParams(
            collective_id=0, has_side_effects=True, vmem_limit_bytes=56 * 1024 * 1024
        ),
        name="lent_attention",
    )(
        home_len, lend_request, lend_blocks, q, nk, nv,
        home_keys, home_values, piece_keys, piece_values, out_weight,
    )
    out = out.reshape(reqs, cols // HD, steps, HD).transpose(0, 2, 1, 3)
    return out.reshape(reqs, steps, cols)


def solution(mesh):
    placed = (
        P("pool", None, "tp"),
        P("pool", None, "tp"),
        P("pool", None, "tp"),
        P("pool", None, "tp"),
        P("pool", None, "tp"),
        P("pool"),
        P("pool", None, "tp"),
        P("pool", None, "tp"),
        P("pool"),
        P("pool"),
        P("tp", None),
    )
    return jax.shard_map(
        per_device, mesh=mesh, in_specs=placed, out_specs=P("pool", None, "tp"), check_vma=False
    )
```

```python
import functools
import math

import jax
import jax.numpy as jnp
from jax import lax
from jax.experimental import pallas as pl
from jax.experimental.pallas import tpu as pltpu
from jax.sharding import PartitionSpec as P

QH = 64
KVH = 8
HD = 128
BLOCK = 128
MASKED = -1e30
MESH = pl.DeviceIdType.MESH
F32 = jnp.float32
BF16 = jnp.bfloat16
COEF = math.log2(math.e) / math.sqrt(HD)


def nt(a, b):
    return lax.dot_general(a, b, (((1,), (1,)), ((), ())), preferred_element_type=F32)


def nn(a, b):
    return lax.dot_general(a, b, (((1,), (0,)), ((), ())), preferred_element_type=F32)


def iota(shape, dim):
    return lax.broadcasted_iota(jnp.int32, shape, dim)


def wide_query(q):
    half = q.shape[0] // 2
    zero = jnp.zeros((half, HD), BF16)
    return jnp.concatenate(
        [
            jnp.concatenate([q[:half], zero], axis=1),
            jnp.concatenate([zero, q[half:]], axis=1),
        ],
        axis=0,
    )


def head_shares(q, keys, valid_len):
    scores = nt(q, keys)
    scores = jnp.where(iota(scores.shape, 1) < valid_len, scores, MASKED)
    top = jnp.max(scores, axis=1, keepdims=True)
    shares = jnp.exp2((scores - top) * COEF)
    summed = jnp.sum(shares, axis=1, keepdims=True)
    return shares.astype(BF16), summed, top * COEF + jnp.log2(summed)


def kernel(
    n, t,
    hlen_h, lreq_h, lblk_h, q_h, nk_h, nv_h, hk_h, hv_h, pk_h, pv_h, w_h,
    out_ref,
    hlen, lreq, lblk, q_v, nk_v, nv_v, hk_v, hv_v, pk_v, pv_v, w_v,
    sn_v, tab_s, tab_r, inv_v, inv_s,
    qs0_v, qs1_v, qr0_v, qr1_v, res_v, sh_v, rs0_v, rs1_v, rr0_v, rr1_v, ls_v, lr_v,
    ho_v, hs_v, hn_v, hl_c, pl_c, e_v, t_v, a0_v, a1_v, acc_v, ps_v, pr_v,
    in_sem, home_sem, w_sem, send_sem, recv_sem, rsend_sem, rrecv_sem,
):
    me = lax.axis_index("pool")
    tp = lax.axis_index("tp")
    reqs, rows, _ = q_v.shape
    slots = pk_v.shape[0]
    steps = 4
    home_chunks = home_sem.shape[1]
    per_chunk = reqs // home_chunks
    cols = w_v.shape[2]
    part_rows = rows // 2
    deep = a0_v.shape[1]
    qs, qr = (qs0_v, qs1_v), (qr0_v, qr1_v)
    rs, rr = (rs0_v, rs1_v), (rr0_v, rr1_v)

    def pool_peer(d):
        return jnp.where(me + d >= n, me + d - n, me + d)

    def tp_peer(d):
        return lax.rem(tp + d, t)

    barrier = pltpu.get_barrier_semaphore()

    for d in range(1, n):
        pl.semaphore_signal(
            barrier, inc=1, device_id={"pool": pool_peer(d)}, device_id_type=MESH
        )
    for d in range(1, t):
        pl.semaphore_signal(
            barrier, inc=1, device_id={"tp": tp_peer(d)}, device_id_type=MESH
        )

    small = [
        pltpu.make_async_copy(src, dst, in_sem.at[i])
        for i, (src, dst) in enumerate(
            [
                (q_h, q_v), (nk_h, nk_v), (nv_h, nv_v), (pk_h, pk_v), (pv_h, pv_v),
                (lreq_h, lreq), (hlen_h, hlen), (lblk_h, lblk),
            ]
        )
    ]
    for i in (5, 6, 7, 0, 1, 2):
        small[i].start()
    home = []
    for c in range(home_chunks):
        part = pl.ds(c * per_chunk, per_chunk)
        home.append(
            [
                pltpu.make_async_copy(hk_h.at[part], hk_v.at[part], home_sem.at[0, c]),
                pltpu.make_async_copy(hv_h.at[part], hv_v.at[part], home_sem.at[1, c]),
            ]
        )
    for c in range(home_chunks):
        home[c][0].start()
        home[c][1].start()
    small[3].start()
    small[4].start()
    order = [2, 1, 3, 0]
    weights = []
    for i, d in enumerate(order):
        column = pl.multiple_of(tp_peer(d) * cols, cols)
        weights.append(
            pltpu.make_async_copy(w_h.at[:, pl.ds(column, cols)], w_v.at[i], w_sem.at[i])
        )

    for i in (5, 6, 7):
        small[i].wait()
    owner_id = iota((n, 128), 0)
    wanted = jnp.full((n, 128), -1, jnp.int32)
    slot_of = jnp.zeros((n, 128), jnp.int32)
    for l in range(slots):
        request = lreq[l]
        owner = request // reqs
        hit = owner_id == owner
        wanted = jnp.where(hit, request - owner * reqs, wanted)
        slot_of = jnp.where(hit, l, slot_of)
    tab_s[...] = wanted.reshape(n, 1, 128)
    inv_v[...] = slot_of.reshape(n, 1, 128)

    def remote(phase, src, dst, d):
        return pltpu.make_async_remote_copy(
            src_ref=src,
            dst_ref=dst,
            send_sem=send_sem.at[phase],
            recv_sem=recv_sem.at[phase],
            device_id={"pool": pool_peer(d)},
            device_id_type=MESH,
        )

    def all_of(phase, buffer):
        part = buffer.at[pl.ds(0, n - 1)]
        return remote(phase, part, part, 1)

    pl.semaphore_wait(barrier, n - 1 + t - 1)

    for d in range(1, n):
        remote(0, tab_s.at[pool_peer(d)], tab_r.at[me], d).start()
    tab_r[me] = tab_s[me]

    for copy in small[:3]:
        copy.wait()
    sn_v[...] = nt(q_v[...].reshape(reqs * rows, HD), nk_v[...]).reshape(reqs, rows, HD)
    t_row = iota(t_v.shape, 0)
    t_col = iota(t_v.shape, 1)
    t_v[...] = jnp.where(
        t_row == (t_col // 128) * 16 + t_col % 16, 1.0, 0.0
    ).astype(BF16)
    hl_c[...] = jnp.zeros(hl_c.shape, F32)
    pl_c[...] = jnp.zeros(pl_c.shape, F32)
    lane = iota((rows, 128), 1)
    row = iota((rows, 128), 0)

    def home_part(c, between):
        home[c][0].wait()
        total = hl_c[0:rows]
        sums = []
        for j in range(per_chunk):
            r = c * per_chunk + j
            low = r * (2 * steps) + (row // (rows // 2)) * steps
            seen = (lane >= low) & (lane <= low + row % steps)
            new_scores = jnp.where(seen, sn_v[r], MASKED)
            scores = nt(wide_query(q_v[r]), hk_v[r])
            scores = jnp.where(iota(scores.shape, 1) < hlen[r], scores, MASKED)
            top = jnp.maximum(
                jnp.max(scores, axis=1, keepdims=True),
                jnp.max(new_scores, axis=1, keepdims=True),
            )
            shares = jnp.exp2((scores - top) * COEF)
            new_shares = jnp.exp2((new_scores - top) * COEF)
            summed = jnp.sum(shares, axis=1, keepdims=True) + jnp.sum(
                new_shares, axis=1, keepdims=True
            )
            hs_v[j] = shares.astype(BF16)
            hn_v[j] = new_shares.astype(BF16)
            sums.append(summed)
            total = jnp.where(lane == r, top * COEF + jnp.log2(summed), total)
            between(j)
        hl_c[0:rows] = total
        home[c][1].wait()
        for j in range(per_chunk):
            r = c * per_chunk + j
            both = nn(hs_v[j], hv_v[r])
            out = jnp.concatenate([both[:part_rows, :HD], both[part_rows:, HD:]], axis=0)
            out = out + nn(hn_v[j], nv_v[...])
            ho_v[r] = (out / sums[j]).astype(BF16)

    def nothing(j):
        pass

    home_part(0, nothing)
    home_part(1, nothing)

    all_of(0, tab_r).wait_recv()

    picks = [jnp.maximum(tab_r[pool_peer(d), 0, 0], 0) for d in range(1, n)]
    mine = jnp.maximum(tab_r[me, 0, 0], 0)
    halves = [slice(0, part_rows), slice(part_rows, rows)]

    def send_query(k, d):
        peer = pool_peer(d)
        qs[k][peer] = q_v[picks[d - 1], halves[k]]
        remote(1 + k, qs[k].at[peer], qr[k].at[me], d).start()

    for k in range(2):
        qr[k][me] = q_v[mine, halves[k]]
    for d in range(1, n):
        send_query(0, d)
    for copy in weights:
        copy.start()

    def query_sends(j):
        for d in range(max(1, j * 8), j * 8 + 8):
            send_query(1, d)

    home_part(2, query_sends)
    home_part(3, nothing)
    for d in range(n):
        inv_s[d] = inv_v[pool_peer(d), 0, 0]

    small[3].wait()
    small[4].wait()
    part_lane = iota((part_rows, 128), 1)

    def send_result(k, d):
        peer = pool_peer(d)
        rs[k][peer] = res_v[inv_s[d], halves[k]]
        remote(4 + k, rs[k].at[peer], rr[k].at[me], d).start()

    def send_lse(d):
        remote(3, ls_v.at[pool_peer(d)], lr_v.at[me], d).start()

    for k in range(2):
        all_of(1 + k, qr[k]).wait_recv()
        width = slice(k * HD, k * HD + HD)
        total = jnp.zeros((part_rows, 128), F32)
        sums = []
        for l in range(slots):
            owner = lreq[l] // reqs
            shares, summed, lse = head_shares(qr[k][owner], pk_v[l, :, width], lblk[l] * BLOCK)
            sh_v[l] = shares
            sums.append(summed)
            total = jnp.where(part_lane == owner, lse, total)
            if k == 1:
                for d in (2 * l, 2 * l + 1):
                    if d > 0:
                        send_result(0, d)
        pl_c[halves[k]] = total
        if k == 1:
            ls_v[...] = pl_c[...].T[0:n].reshape(n, 1, 128)
            lr_v[me] = ls_v[me]
        for l in range(slots):
            out = nn(sh_v[l], pv_v[l, :, width])
            res_v[l, halves[k]] = (out / sums[l]).astype(BF16)
            if k == 1:
                for d in (2 * l, 2 * l + 1):
                    if d > 0:
                        send_lse(d)
        rr[k][me] = res_v[inv_s[0], halves[k]]
    eight = iota((8, 128), 1) // 16 == iota((8, 128), 0)
    local = tab_r[...].reshape(n, 128)
    parts = n + reqs
    seg = jnp.concatenate([local, iota((reqs, 128), 0)], axis=0)
    seg_lane = jnp.concatenate(
        [
            jnp.sum(jnp.where(eight, seg[c * 8 : c * 8 + 8], 0), axis=0, keepdims=True)
            for c in range(parts // 8)
        ],
        axis=1,
    )
    block = (16, parts * 16)
    b_row, b_col = iota(block, 0), iota(block, 1)
    head_step = b_col % 16 - b_row % steps
    owner_row = seg_lane - b_row // steps
    for i in range(16):
        same = (head_step == i // 4 * steps) & (owner_row == i % 4 * 4)
        e_v[i] = jnp.where(same, 1.0, 0.0).astype(BF16)
        for d in (2 * i, 2 * i + 1):
            if d > 0:
                send_result(1, d)
    all_of(3, lr_v).wait_recv()
    lse = jnp.concatenate([lr_v[...].reshape(n, 128), hl_c[...].T[0:reqs]], axis=0)
    big = lse
    for r in range(reqs):
        hit = seg == r
        big = jnp.where(hit, jnp.max(jnp.where(hit, lse, MASKED), axis=0, keepdims=True), big)
    share = jnp.where(seg >= 0, jnp.exp2(lse - big), 0.0)
    total = jnp.ones_like(share)
    for r in range(reqs):
        hit = seg == r
        total = jnp.where(
            hit, jnp.sum(jnp.where(hit, share, 0.0), axis=0, keepdims=True), total
        )
    spread = nn((share / total).astype(BF16), t_v[...])

    def merge(k, a_v):
        all_of(4 + k, rr[k]).wait_recv()
        for g in range(part_rows // 16):
            wide = (k * (part_rows // 16) + g) * 128
            along = jnp.concatenate(
                [
                    jnp.sum(
                        jnp.where(
                            eight, spread[c * 8 : c * 8 + 8, wide : wide + 128], 0.0
                        ),
                        axis=0,
                        keepdims=True,
                    )
                    for c in range(parts // 8)
                ],
                axis=1,
            )
            along = jnp.broadcast_to(along, block).astype(BF16)
            left = (e_v[...] * along[None]).reshape(256, parts * 16)
            group = slice(g * 16, g * 16 + 16)
            own = slice(k * part_rows + g * 16, k * part_rows + g * 16 + 16)
            right = jnp.concatenate(
                [rr[k][:, group].reshape(n * 16, HD), ho_v[:, own].reshape(reqs * 16, HD)],
                axis=0,
            )
            merged = nn(left, right).astype(BF16)
            for h in range(4):
                head = g * 4 + h
                a_v[:, head * HD : head * HD + HD] = merged[h * rows : h * rows + rows]

    merge(0, a0_v)
    for i in range(t):
        weights[i].wait()
        acc_v[i] = nn(a0_v[...], w_v[i, 0:deep])
    merge(1, a1_v)

    def projected(i):
        return acc_v[i] + nn(a1_v[...], w_v[i, deep : 2 * deep])

    half = cols // 2

    def to_neighbour(i, src, side):
        return pltpu.make_async_remote_copy(
            src_ref=src,
            dst_ref=pr_v.at[i],
            send_sem=rsend_sem.at[i],
            recv_sem=rrecv_sem.at[i],
            device_id={"tp": tp_peer(side)},
            device_id_type=MESH,
        )

    up, down = 1, t - 1
    hops = [
        to_neighbour(i, ps_v.at[i], side)
        for i, side in enumerate([up, down, up, down, up, down])
    ]
    for i in range(2):
        at = slice(i * half, i * half + half)
        value = acc_v[0, :, at] + nn(a1_v[...], w_v[0, deep : 2 * deep, at])
        ps_v[i] = value.astype(BF16)
        hops[i].start()
    above = projected(1)
    ps_v[2] = above[:, half:].astype(BF16)
    hops[2].start()
    acc_v[1, :, :half] = above[:, :half]
    below = projected(2)
    ps_v[3] = below[:, :half].astype(BF16)
    hops[3].start()
    hops[0].wait_recv()
    ps_v[4] = (acc_v[1, :, :half] + pr_v[0].astype(F32)).astype(BF16)
    hops[4].start()
    hops[1].wait_recv()
    ps_v[5] = (below[:, half:] + pr_v[1].astype(F32)).astype(BF16)
    hops[5].start()
    acc_v[3] = projected(3)
    for i in range(2, 6):
        hops[i].wait_recv()
    from_below = jnp.concatenate([pr_v[4], pr_v[2]], axis=1).astype(F32)
    from_above = jnp.concatenate([pr_v[3], pr_v[5]], axis=1).astype(F32)
    result = acc_v[3] + from_below + from_above

    first = iota((8, 8, HD), 1) < 4
    for g in range(2):
        even, odd = [], []
        for k in range(2):
            c = (g * 2 + k) * 2 * HD
            left = result[:, c : c + HD].reshape(8, 8, HD)
            right = result[:, c + HD : c + 2 * HD].reshape(8, 8, HD)
            even.append(jnp.where(first, left, pltpu.roll(right, 4, 1)))
            odd.append(jnp.where(first, pltpu.roll(left, 4, 1), right))
        for k, both in enumerate([even, odd]):
            out_ref[:, k, g * 16 : g * 16 + 16] = jnp.concatenate(both, axis=1).astype(BF16)

    all_of(0, tab_s).wait_send()
    for k in range(2):
        all_of(1 + k, qs[k]).wait_send()
        all_of(4 + k, rs[k]).wait_send()
    all_of(3, ls_v).wait_send()
    for hop in hops:
        hop.wait_send()


def per_device(
    queries, home_keys, home_values, new_keys, new_values, home_len,
    piece_keys, piece_values, lend_request, lend_blocks, out_weight,
):
    n = lax.axis_size("pool")
    t = lax.axis_size("tp")
    reqs, steps, features = queries.shape
    heads = features // HD
    kv = new_keys.shape[2] // HD
    rows = heads * steps
    slots, piece = piece_keys.shape[:2]
    cols = out_weight.shape[1] // t

    def head_rows(x):
        count = x.shape[2] // HD
        return x.reshape(reqs, steps, count, HD).transpose(0, 2, 1, 3)

    q = head_rows(queries).reshape(reqs, rows, HD)
    nk = head_rows(new_keys).reshape(reqs * kv * steps, HD)
    nv = head_rows(new_values).reshape(reqs * kv * steps, HD)
    hbm = pl.BlockSpec(memory_space=pl.ANY)
    chunks = 4
    vmem = pltpu.VMEM
    out = pl.pallas_call(
        functools.partial(kernel, n, t),
        out_shape=vmem((reqs // 2, 2, cols // HD * steps, HD), BF16),
        in_specs=[hbm] * 11,
        out_specs=pl.BlockSpec(memory_space=pltpu.VMEM),
        scratch_shapes=[
            *[pltpu.SMEM((reqs,), jnp.int32)] * 3,
            vmem(q.shape, BF16),
            vmem(nk.shape, BF16),
            vmem(nv.shape, BF16),
            vmem(home_keys.shape, BF16),
            vmem(home_values.shape, BF16),
            vmem(piece_keys.shape, BF16),
            vmem(piece_values.shape, BF16),
            vmem((t, features, cols), BF16),
            vmem((reqs, rows, 128), F32),
            vmem((n, 1, 128), jnp.int32),
            vmem((n, 1, 128), jnp.int32),
            vmem((n, 1, 128), jnp.int32),
            pltpu.SMEM((n,), jnp.int32),
            *[vmem((n, rows // 2, HD), BF16)] * 4,
            vmem((slots, rows, HD), BF16),
            vmem((slots, rows // 2, piece), BF16),
            *[vmem((n, rows // 2, HD), BF16)] * 4,
            *[vmem((n, 1, 128), F32)] * 2,
            vmem((reqs, rows, HD), BF16),
            vmem((reqs // chunks, rows, home_keys.shape[1]), BF16),
            vmem((reqs // chunks, rows, 128), BF16),
            *[vmem((128, 128), F32)] * 2,
            vmem((16, 16, (n + reqs) * 16), BF16),
            vmem((128, (rows // 16) * 128), BF16),
            *[vmem((reqs * steps, features // 2), BF16)] * 2,
            vmem((t, reqs * steps, cols), F32),
            vmem((6, reqs * steps, cols // 2), BF16),
            vmem((6, reqs * steps, cols // 2), BF16),
            pltpu.SemaphoreType.DMA((8,)),
            pltpu.SemaphoreType.DMA((2, chunks)),
            pltpu.SemaphoreType.DMA((t,)),
            pltpu.SemaphoreType.DMA((6,)),
            pltpu.SemaphoreType.DMA((6,)),
            pltpu.SemaphoreType.DMA((6,)),
            pltpu.SemaphoreType.DMA((6,)),
        ],
        compiler_params=pltpu.CompilerParams(
            collective_id=0, has_side_effects=True, vmem_limit_bytes=56 * 1024 * 1024
        ),
        name="lent_attention",
    )(
        home_len, lend_request, lend_blocks, q, nk, nv,
        home_keys, home_values, piece_keys, piece_values, out_weight,
    )
    out = out.reshape(reqs, cols // HD, steps, HD).transpose(0, 2, 1, 3)
    return out.reshape(reqs, steps, cols)


def solution(mesh):
    placed = (
        P("pool", None, "tp"),
        P("pool", None, "tp"),
        P("pool", None, "tp"),
        P("pool", None, "tp"),
        P("pool", None, "tp"),
        P("pool"),
        P("pool", None, "tp"),
        P("pool", None, "tp"),
        P("pool"),
        P("pool"),
        P("tp", None),
    )
    return jax.shard_map(
        per_device, mesh=mesh, in_specs=placed, out_specs=P("pool", None, "tp"), check_vma=False
    )
```

```python
import functools
import math

import jax
import jax.numpy as jnp
from jax import lax
from jax.experimental import pallas as pl
from jax.experimental.pallas import tpu as pltpu
from jax.sharding import PartitionSpec as P

QH = 64
KVH = 8
HD = 128
BLOCK = 128
MASKED = -1e30
MESH = pl.DeviceIdType.MESH
F32 = jnp.float32
BF16 = jnp.bfloat16
COEF = math.log2(math.e) / math.sqrt(HD)


def hops(d):
    dy, dx = d // 8, d // 2 % 4
    return min(dy, 4 - dy) + min(dx, 4 - dx)


FAR_FIRST = sorted(range(1, 32), key=lambda d: -hops(d))


def nt(a, b):
    return lax.dot_general(a, b, (((1,), (1,)), ((), ())), preferred_element_type=F32)


def nn(a, b):
    return lax.dot_general(a, b, (((1,), (0,)), ((), ())), preferred_element_type=F32)


def iota(shape, dim):
    return lax.broadcasted_iota(jnp.int32, shape, dim)


def wide_query(q):
    half = q.shape[0] // 2
    zero = jnp.zeros((half, HD), BF16)
    return jnp.concatenate(
        [
            jnp.concatenate([q[:half], zero], axis=1),
            jnp.concatenate([zero, q[half:]], axis=1),
        ],
        axis=0,
    )


def head_shares(q, keys, valid_len):
    scores = nt(q, keys)
    scores = jnp.where(iota(scores.shape, 1) < valid_len, scores, MASKED)
    top = jnp.max(scores, axis=1, keepdims=True)
    shares = jnp.exp2((scores - top) * COEF)
    summed = jnp.sum(shares, axis=1, keepdims=True)
    return shares.astype(BF16), summed, top * COEF + jnp.log2(summed)


def kernel(
    n, t,
    hlen_h, lreq_h, lblk_h, q_h, nk_h, nv_h, hk_h, hv_h, pk_h, pv_h, w_h,
    out_ref,
    hlen, lreq, lblk, q_v, nk_v, nv_v, hk_v, hv_v, pk_v, pv_v, w_v,
    sn_v, tab_s, tab_r, inv_v, inv_s,
    qs0_v, qs1_v, qr0_v, qr1_v, res_v, sh_v, rs0_v, rs1_v, rr0_v, rr1_v, ls_v, lr_v,
    ho_v, hs_v, hn_v, hl_c, pl_c, e_v, t_v, a0_v, a1_v, acc_v, ps_v, pr_v,
    in_sem, home_sem, w_sem, send_sem, recv_sem, rsend_sem, rrecv_sem,
):
    me = lax.axis_index("pool")
    tp = lax.axis_index("tp")
    reqs, rows, _ = q_v.shape
    slots = pk_v.shape[0]
    steps = 4
    home_chunks = home_sem.shape[1]
    per_chunk = reqs // home_chunks
    cols = w_v.shape[2]
    part_rows = rows // 2
    deep = a0_v.shape[1]
    qs, qr = (qs0_v, qs1_v), (qr0_v, qr1_v)
    rs, rr = (rs0_v, rs1_v), (rr0_v, rr1_v)

    def pool_peer(d):
        return jnp.where(me + d >= n, me + d - n, me + d)

    def tp_peer(d):
        return lax.rem(tp + d, t)

    barrier = pltpu.get_barrier_semaphore()

    for d in range(1, t):
        pl.semaphore_signal(
            barrier, inc=1, device_id={"tp": tp_peer(d)}, device_id_type=MESH
        )
    for d in FAR_FIRST:
        pl.semaphore_signal(
            barrier, inc=1, device_id={"pool": pool_peer(d)}, device_id_type=MESH
        )

    small = [
        pltpu.make_async_copy(src, dst, in_sem.at[i])
        for i, (src, dst) in enumerate(
            [
                (q_h, q_v), (nk_h, nk_v), (nv_h, nv_v), (pk_h, pk_v), (pv_h, pv_v),
                (lreq_h, lreq), (hlen_h, hlen), (lblk_h, lblk),
            ]
        )
    ]
    for i in (5, 6, 7, 0, 1, 2):
        small[i].start()
    home = []
    for c in range(home_chunks):
        part = pl.ds(c * per_chunk, per_chunk)
        home.append(
            [
                pltpu.make_async_copy(hk_h.at[part], hk_v.at[part], home_sem.at[0, c]),
                pltpu.make_async_copy(hv_h.at[part], hv_v.at[part], home_sem.at[1, c]),
            ]
        )
    for c in range(home_chunks):
        home[c][0].start()
        home[c][1].start()
    small[3].start()
    small[4].start()
    order = [2, 1, 3, 0]
    weights = []
    for i, d in enumerate(order):
        column = pl.multiple_of(tp_peer(d) * cols, cols)
        weights.append(
            pltpu.make_async_copy(w_h.at[:, pl.ds(column, cols)], w_v.at[i], w_sem.at[i])
        )

    for i in (5, 6, 7):
        small[i].wait()
    owner_id = iota((n, 128), 0)
    wanted = jnp.full((n, 128), -1, jnp.int32)
    slot_of = jnp.zeros((n, 128), jnp.int32)
    for l in range(slots):
        request = lreq[l]
        owner = request // reqs
        hit = owner_id == owner
        wanted = jnp.where(hit, request - owner * reqs, wanted)
        slot_of = jnp.where(hit, l, slot_of)
    tab_s[...] = wanted.reshape(n, 1, 128)
    inv_v[...] = slot_of.reshape(n, 1, 128)

    def remote(phase, src, dst, d):
        return pltpu.make_async_remote_copy(
            src_ref=src,
            dst_ref=dst,
            send_sem=send_sem.at[phase],
            recv_sem=recv_sem.at[phase],
            device_id={"pool": pool_peer(d)},
            device_id_type=MESH,
        )

    def all_of(phase, buffer):
        part = buffer.at[pl.ds(0, n - 1)]
        return remote(phase, part, part, 1)

    pl.semaphore_wait(barrier, n - 1 + t - 1)

    for d in FAR_FIRST:
        remote(0, tab_s.at[pool_peer(d)], tab_r.at[me], d).start()
    tab_r[me] = tab_s[me]

    for copy in small[:3]:
        copy.wait()
    sn_v[...] = nt(q_v[...].reshape(reqs * rows, HD), nk_v[...]).reshape(reqs, rows, HD)
    t_row = iota(t_v.shape, 0)
    t_col = iota(t_v.shape, 1)
    t_v[...] = jnp.where(
        t_row == (t_col // 128) * 16 + t_col % 16, 1.0, 0.0
    ).astype(BF16)
    hl_c[...] = jnp.zeros(hl_c.shape, F32)
    pl_c[...] = jnp.zeros(pl_c.shape, F32)
    lane = iota((rows, 128), 1)
    row = iota((rows, 128), 0)

    def home_part(c, between):
        home[c][0].wait()
        total = hl_c[0:rows]
        sums = []
        for j in range(per_chunk):
            r = c * per_chunk + j
            low = r * (2 * steps) + (row // (rows // 2)) * steps
            seen = (lane >= low) & (lane <= low + row % steps)
            new_scores = jnp.where(seen, sn_v[r], MASKED)
            scores = nt(wide_query(q_v[r]), hk_v[r])
            scores = jnp.where(iota(scores.shape, 1) < hlen[r], scores, MASKED)
            top = jnp.maximum(
                jnp.max(scores, axis=1, keepdims=True),
                jnp.max(new_scores, axis=1, keepdims=True),
            )
            shares = jnp.exp2((scores - top) * COEF)
            new_shares = jnp.exp2((new_scores - top) * COEF)
            summed = jnp.sum(shares, axis=1, keepdims=True) + jnp.sum(
                new_shares, axis=1, keepdims=True
            )
            hs_v[j] = shares.astype(BF16)
            hn_v[j] = new_shares.astype(BF16)
            sums.append(summed)
            total = jnp.where(lane == r, top * COEF + jnp.log2(summed), total)
            between(j)
        hl_c[0:rows] = total
        home[c][1].wait()
        for j in range(per_chunk):
            r = c * per_chunk + j
            both = nn(hs_v[j], hv_v[r])
            out = jnp.concatenate([both[:part_rows, :HD], both[part_rows:, HD:]], axis=0)
            out = out + nn(hn_v[j], nv_v[...])
            ho_v[r] = (out / sums[j]).astype(BF16)

    def nothing(j):
        pass

    home_part(0, nothing)
    home_part(1, nothing)

    all_of(0, tab_r).wait_recv()

    picks = {d: jnp.maximum(tab_r[pool_peer(d), 0, 0], 0) for d in FAR_FIRST}
    mine = jnp.maximum(tab_r[me, 0, 0], 0)
    halves = [slice(0, part_rows), slice(part_rows, rows)]

    def send_query(k, d):
        peer = pool_peer(d)
        qs[k][peer] = q_v[picks[d], halves[k]]
        remote(1 + k, qs[k].at[peer], qr[k].at[me], d).start()

    for k in range(2):
        qr[k][me] = q_v[mine, halves[k]]
    for d in FAR_FIRST:
        send_query(0, d)
    for copy in weights:
        copy.start()

    def query_sends(j):
        for d in FAR_FIRST[j * 8 : j * 8 + 8]:
            send_query(1, d)

    home_part(2, query_sends)
    home_part(3, nothing)
    for d in range(n):
        inv_s[d] = inv_v[pool_peer(d), 0, 0]

    small[3].wait()
    small[4].wait()
    part_lane = iota((part_rows, 128), 1)

    def send_result(k, d):
        peer = pool_peer(d)
        rs[k][peer] = res_v[inv_s[d], halves[k]]
        remote(4 + k, rs[k].at[peer], rr[k].at[me], d).start()

    def send_lse(d):
        remote(3, ls_v.at[pool_peer(d)], lr_v.at[me], d).start()

    for k in range(2):
        all_of(1 + k, qr[k]).wait_recv()
        width = slice(k * HD, k * HD + HD)
        total = jnp.zeros((part_rows, 128), F32)
        sums = []
        for l in range(slots):
            owner = lreq[l] // reqs
            shares, summed, lse = head_shares(qr[k][owner], pk_v[l, :, width], lblk[l] * BLOCK)
            sh_v[l] = shares
            sums.append(summed)
            total = jnp.where(part_lane == owner, lse, total)
            if k == 1:
                for d in FAR_FIRST[2 * l : 2 * l + 2]:
                    send_result(0, d)
        pl_c[halves[k]] = total
        if k == 1:
            ls_v[...] = pl_c[...].T[0:n].reshape(n, 1, 128)
            lr_v[me] = ls_v[me]
        for l in range(slots):
            out = nn(sh_v[l], pv_v[l, :, width])
            res_v[l, halves[k]] = (out / sums[l]).astype(BF16)
            if k == 1:
                for d in FAR_FIRST[2 * l : 2 * l + 2]:
                    send_lse(d)
        rr[k][me] = res_v[inv_s[0], halves[k]]
    eight = iota((8, 128), 1) // 16 == iota((8, 128), 0)
    local = tab_r[...].reshape(n, 128)
    parts = n + reqs
    seg = jnp.concatenate([local, iota((reqs, 128), 0)], axis=0)
    seg_lane = jnp.concatenate(
        [
            jnp.sum(jnp.where(eight, seg[c * 8 : c * 8 + 8], 0), axis=0, keepdims=True)
            for c in range(parts // 8)
        ],
        axis=1,
    )
    block = (16, parts * 16)
    b_row, b_col = iota(block, 0), iota(block, 1)
    head_step = b_col % 16 - b_row % steps
    owner_row = seg_lane - b_row // steps
    for i in range(16):
        same = (head_step == i // 4 * steps) & (owner_row == i % 4 * 4)
        e_v[i] = jnp.where(same, 1.0, 0.0).astype(BF16)
        for d in FAR_FIRST[2 * i : 2 * i + 2]:
            send_result(1, d)
    all_of(3, lr_v).wait_recv()
    lse = jnp.concatenate([lr_v[...].reshape(n, 128), hl_c[...].T[0:reqs]], axis=0)
    big = lse
    for r in range(reqs):
        hit = seg == r
        big = jnp.where(hit, jnp.max(jnp.where(hit, lse, MASKED), axis=0, keepdims=True), big)
    share = jnp.where(seg >= 0, jnp.exp2(lse - big), 0.0)
    total = jnp.ones_like(share)
    for r in range(reqs):
        hit = seg == r
        total = jnp.where(
            hit, jnp.sum(jnp.where(hit, share, 0.0), axis=0, keepdims=True), total
        )
    spread = nn((share / total).astype(BF16), t_v[...])

    def merge(k, a_v):
        all_of(4 + k, rr[k]).wait_recv()
        for g in range(part_rows // 16):
            wide = (k * (part_rows // 16) + g) * 128
            along = jnp.concatenate(
                [
                    jnp.sum(
                        jnp.where(
                            eight, spread[c * 8 : c * 8 + 8, wide : wide + 128], 0.0
                        ),
                        axis=0,
                        keepdims=True,
                    )
                    for c in range(parts // 8)
                ],
                axis=1,
            )
            along = jnp.broadcast_to(along, block).astype(BF16)
            left = (e_v[...] * along[None]).reshape(256, parts * 16)
            group = slice(g * 16, g * 16 + 16)
            own = slice(k * part_rows + g * 16, k * part_rows + g * 16 + 16)
            right = jnp.concatenate(
                [rr[k][:, group].reshape(n * 16, HD), ho_v[:, own].reshape(reqs * 16, HD)],
                axis=0,
            )
            merged = nn(left, right).astype(BF16)
            for h in range(4):
                head = g * 4 + h
                a_v[:, head * HD : head * HD + HD] = merged[h * rows : h * rows + rows]

    merge(0, a0_v)
    for i in range(t):
        weights[i].wait()
        acc_v[i] = nn(a0_v[...], w_v[i, 0:deep])
    merge(1, a1_v)

    half = cols // 2
    left, right = slice(0, half), slice(half, cols)

    def projected(i, at):
        return acc_v[i, :, at] + nn(a1_v[...], w_v[i, deep : 2 * deep, at])

    def to_neighbour(i, src, side):
        return pltpu.make_async_remote_copy(
            src_ref=src,
            dst_ref=pr_v.at[i],
            send_sem=rsend_sem.at[i],
            recv_sem=rrecv_sem.at[i],
            device_id={"tp": tp_peer(side)},
            device_id_type=MESH,
        )

    up, down = 1, t - 1
    ring = [
        to_neighbour(i, ps_v.at[i], side)
        for i, side in enumerate([up, down, up, down, up, down])
    ]
    def send(i, value):
        ps_v[i] = value.astype(BF16)
        ring[i].start()

    send(0, projected(0, left))
    send(1, projected(0, right))
    send(2, projected(1, right))
    send(3, projected(2, left))
    above = projected(1, left)
    ring[0].wait_recv()
    send(4, above + pr_v[0].astype(F32))
    below = projected(2, right)
    ring[1].wait_recv()
    send(5, below + pr_v[1].astype(F32))
    own = jnp.concatenate([projected(3, left), projected(3, right)], axis=1)
    for i in range(2, 6):
        ring[i].wait_recv()
    from_below = jnp.concatenate([pr_v[4], pr_v[2]], axis=1).astype(F32)
    from_above = jnp.concatenate([pr_v[3], pr_v[5]], axis=1).astype(F32)
    result = own + from_below + from_above

    first = iota((8, 8, HD), 1) < 4
    for g in range(2):
        even, odd = [], []
        for k in range(2):
            c = (g * 2 + k) * 2 * HD
            left = result[:, c : c + HD].reshape(8, 8, HD)
            right = result[:, c + HD : c + 2 * HD].reshape(8, 8, HD)
            even.append(jnp.where(first, left, pltpu.roll(right, 4, 1)))
            odd.append(jnp.where(first, pltpu.roll(left, 4, 1), right))
        for k, both in enumerate([even, odd]):
            out_ref[:, k, g * 16 : g * 16 + 16] = jnp.concatenate(both, axis=1).astype(BF16)

    all_of(0, tab_s).wait_send()
    for k in range(2):
        all_of(1 + k, qs[k]).wait_send()
        all_of(4 + k, rs[k]).wait_send()
    all_of(3, ls_v).wait_send()
    for copy in ring:
        copy.wait_send()


def per_device(
    queries, home_keys, home_values, new_keys, new_values, home_len,
    piece_keys, piece_values, lend_request, lend_blocks, out_weight,
):
    n = lax.axis_size("pool")
    t = lax.axis_size("tp")
    reqs, steps, features = queries.shape
    heads = features // HD
    kv = new_keys.shape[2] // HD
    rows = heads * steps
    slots, piece = piece_keys.shape[:2]
    cols = out_weight.shape[1] // t

    def head_rows(x):
        count = x.shape[2] // HD
        return x.reshape(reqs, steps, count, HD).transpose(0, 2, 1, 3)

    q = head_rows(queries).reshape(reqs, rows, HD)
    nk = head_rows(new_keys).reshape(reqs * kv * steps, HD)
    nv = head_rows(new_values).reshape(reqs * kv * steps, HD)
    hbm = pl.BlockSpec(memory_space=pl.ANY)
    chunks = 4
    vmem = pltpu.VMEM
    out = pl.pallas_call(
        functools.partial(kernel, n, t),
        out_shape=vmem((reqs // 2, 2, cols // HD * steps, HD), BF16),
        in_specs=[hbm] * 11,
        out_specs=pl.BlockSpec(memory_space=pltpu.VMEM),
        scratch_shapes=[
            *[pltpu.SMEM((reqs,), jnp.int32)] * 3,
            vmem(q.shape, BF16),
            vmem(nk.shape, BF16),
            vmem(nv.shape, BF16),
            vmem(home_keys.shape, BF16),
            vmem(home_values.shape, BF16),
            vmem(piece_keys.shape, BF16),
            vmem(piece_values.shape, BF16),
            vmem((t, features, cols), BF16),
            vmem((reqs, rows, 128), F32),
            vmem((n, 1, 128), jnp.int32),
            vmem((n, 1, 128), jnp.int32),
            vmem((n, 1, 128), jnp.int32),
            pltpu.SMEM((n,), jnp.int32),
            *[vmem((n, rows // 2, HD), BF16)] * 4,
            vmem((slots, rows, HD), BF16),
            vmem((slots, rows // 2, piece), BF16),
            *[vmem((n, rows // 2, HD), BF16)] * 4,
            *[vmem((n, 1, 128), F32)] * 2,
            vmem((reqs, rows, HD), BF16),
            vmem((reqs // chunks, rows, home_keys.shape[1]), BF16),
            vmem((reqs // chunks, rows, 128), BF16),
            *[vmem((128, 128), F32)] * 2,
            vmem((16, 16, (n + reqs) * 16), BF16),
            vmem((128, (rows // 16) * 128), BF16),
            *[vmem((reqs * steps, features // 2), BF16)] * 2,
            vmem((t, reqs * steps, cols), F32),
            vmem((6, reqs * steps, cols // 2), BF16),
            vmem((6, reqs * steps, cols // 2), BF16),
            pltpu.SemaphoreType.DMA((8,)),
            pltpu.SemaphoreType.DMA((2, chunks)),
            pltpu.SemaphoreType.DMA((t,)),
            pltpu.SemaphoreType.DMA((6,)),
            pltpu.SemaphoreType.DMA((6,)),
            pltpu.SemaphoreType.DMA((6,)),
            pltpu.SemaphoreType.DMA((6,)),
        ],
        compiler_params=pltpu.CompilerParams(
            collective_id=0, has_side_effects=True, vmem_limit_bytes=56 * 1024 * 1024
        ),
        name="lent_attention",
    )(
        home_len, lend_request, lend_blocks, q, nk, nv,
        home_keys, home_values, piece_keys, piece_values, out_weight,
    )
    out = out.reshape(reqs, cols // HD, steps, HD).transpose(0, 2, 1, 3)
    return out.reshape(reqs, steps, cols)


def solution(mesh):
    placed = (
        P("pool", None, "tp"),
        P("pool", None, "tp"),
        P("pool", None, "tp"),
        P("pool", None, "tp"),
        P("pool", None, "tp"),
        P("pool"),
        P("pool", None, "tp"),
        P("pool", None, "tp"),
        P("pool"),
        P("pool"),
        P("tp", None),
    )
    return jax.shard_map(
        per_device, mesh=mesh, in_specs=placed, out_specs=P("pool", None, "tp"), check_vma=False
    )
```

```python
import functools
import math

import jax
import jax.numpy as jnp
from jax import lax
from jax.experimental import pallas as pl
from jax.experimental.pallas import tpu as pltpu
from jax.sharding import PartitionSpec as P

QH = 64
KVH = 8
HD = 128
BLOCK = 128
MASKED = -1e30
MESH = pl.DeviceIdType.MESH
F32 = jnp.float32
BF16 = jnp.bfloat16
COEF = math.log2(math.e) / math.sqrt(HD)


def hops(d):
    dy, dx = d // 8, d // 2 % 4
    return min(dy, 4 - dy) + min(dx, 4 - dx)


FAR_FIRST = sorted(range(1, 32), key=lambda d: -hops(d))


def nt(a, b):
    return lax.dot_general(a, b, (((1,), (1,)), ((), ())), preferred_element_type=F32)


def nn(a, b):
    return lax.dot_general(a, b, (((1,), (0,)), ((), ())), preferred_element_type=F32)


def iota(shape, dim):
    return lax.broadcasted_iota(jnp.int32, shape, dim)


def wide_query(q):
    half = q.shape[0] // 2
    zero = jnp.zeros((half, HD), BF16)
    return jnp.concatenate(
        [
            jnp.concatenate([q[:half], zero], axis=1),
            jnp.concatenate([zero, q[half:]], axis=1),
        ],
        axis=0,
    )


def head_shares(q, keys, valid_len):
    scores = nt(q, keys)
    scores = jnp.where(iota(scores.shape, 1) < valid_len, scores, MASKED)
    top = jnp.max(scores, axis=1, keepdims=True)
    shares = jnp.exp2((scores - top) * COEF)
    summed = jnp.sum(shares, axis=1, keepdims=True)
    return shares.astype(BF16), summed, top * COEF + jnp.log2(summed)


def kernel(
    n, t,
    hlen_h, lreq_h, lblk_h, q_h, nk_h, nv_h, hk_h, hv_h, pk_h, pv_h, w_h,
    out_ref,
    hlen, lreq, lblk, q_v, nk_v, nv_v, hk_v, hv_v, pk_v, pv_v, w_v,
    sn_v, tab_s, tab_r, inv_v, inv_s,
    qs0_v, qs1_v, qr0_v, qr1_v, res_v, sh_v, rs0_v, rs1_v, rr0_v, rr1_v, ls_v, lr_v,
    ho_v, hs_v, hn_v, hl_c, pl_c, e_v, t_v, l_v, a0_v, a1_v, acc_v, ps_v, pr_v,
    in_sem, home_sem, w_sem, send_sem, recv_sem, rsend_sem, rrecv_sem,
):
    me = lax.axis_index("pool")
    tp = lax.axis_index("tp")
    reqs, rows, _ = q_v.shape
    slots = pk_v.shape[0]
    steps = 4
    home_chunks = home_sem.shape[1]
    per_chunk = reqs // home_chunks
    cols = w_v.shape[2]
    part_rows = rows // 2
    deep = a0_v.shape[1]
    qs, qr = (qs0_v, qs1_v), (qr0_v, qr1_v)
    rs, rr = (rs0_v, rs1_v), (rr0_v, rr1_v)

    def pool_peer(d):
        return jnp.where(me + d >= n, me + d - n, me + d)

    def tp_peer(d):
        return lax.rem(tp + d, t)

    barrier = pltpu.get_barrier_semaphore()

    for d in range(1, t):
        pl.semaphore_signal(
            barrier, inc=1, device_id={"tp": tp_peer(d)}, device_id_type=MESH
        )
    for d in FAR_FIRST:
        pl.semaphore_signal(
            barrier, inc=1, device_id={"pool": pool_peer(d)}, device_id_type=MESH
        )

    small = [
        pltpu.make_async_copy(src, dst, in_sem.at[i])
        for i, (src, dst) in enumerate(
            [
                (q_h, q_v), (nk_h, nk_v), (nv_h, nv_v), (pk_h, pk_v), (pv_h, pv_v),
                (lreq_h, lreq), (hlen_h, hlen), (lblk_h, lblk),
            ]
        )
    ]
    for i in (5, 6, 7, 0, 1, 2):
        small[i].start()
    home = []
    for c in range(home_chunks):
        part = pl.ds(c * per_chunk, per_chunk)
        home.append(
            [
                pltpu.make_async_copy(hk_h.at[part], hk_v.at[part], home_sem.at[0, c]),
                pltpu.make_async_copy(hv_h.at[part], hv_v.at[part], home_sem.at[1, c]),
            ]
        )
    for c in range(home_chunks):
        home[c][0].start()
        home[c][1].start()
    small[3].start()
    small[4].start()
    order = [2, 1, 3, 0]
    weights = []
    for i, d in enumerate(order):
        column = pl.multiple_of(tp_peer(d) * cols, cols)
        weights.append(
            pltpu.make_async_copy(w_h.at[:, pl.ds(column, cols)], w_v.at[i], w_sem.at[i])
        )

    for i in (5, 6, 7):
        small[i].wait()
    owner_id = iota((n, 128), 0)
    wanted = jnp.full((n, 128), -1, jnp.int32)
    slot_of = jnp.zeros((n, 128), jnp.int32)
    for l in range(slots):
        request = lreq[l]
        owner = request // reqs
        hit = owner_id == owner
        wanted = jnp.where(hit, request - owner * reqs, wanted)
        slot_of = jnp.where(hit, l, slot_of)
    tab_s[...] = wanted.reshape(n, 1, 128)
    inv_v[...] = slot_of.reshape(n, 1, 128)

    def remote(phase, src, dst, d):
        return pltpu.make_async_remote_copy(
            src_ref=src,
            dst_ref=dst,
            send_sem=send_sem.at[phase],
            recv_sem=recv_sem.at[phase],
            device_id={"pool": pool_peer(d)},
            device_id_type=MESH,
        )

    def all_of(phase, buffer):
        part = buffer.at[pl.ds(0, n - 1)]
        return remote(phase, part, part, 1)

    pl.semaphore_wait(barrier, n - 1 + t - 1)

    for d in FAR_FIRST:
        remote(0, tab_s.at[pool_peer(d)], tab_r.at[me], d).start()
    tab_r[me] = tab_s[me]

    for copy in small[:3]:
        copy.wait()
    sn_v[...] = nt(q_v[...].reshape(reqs * rows, HD), nk_v[...]).reshape(reqs, rows, HD)
    t_row = iota(t_v.shape, 0)
    t_col = iota(t_v.shape, 1)
    t_v[...] = jnp.where(
        t_row == (t_col // 128) * 16 + t_col % 16, 1.0, 0.0
    ).astype(BF16)
    hl_c[...] = jnp.zeros(hl_c.shape, F32)
    pl_c[...] = jnp.zeros(pl_c.shape, F32)
    lane = iota((rows, 128), 1)
    row = iota((rows, 128), 0)

    def home_part(c, between):
        home[c][0].wait()
        total = hl_c[0:rows]
        sums = []
        for j in range(per_chunk):
            r = c * per_chunk + j
            low = r * (2 * steps) + (row // (rows // 2)) * steps
            seen = (lane >= low) & (lane <= low + row % steps)
            new_scores = jnp.where(seen, sn_v[r], MASKED)
            scores = nt(wide_query(q_v[r]), hk_v[r])
            scores = jnp.where(iota(scores.shape, 1) < hlen[r], scores, MASKED)
            top = jnp.maximum(
                jnp.max(scores, axis=1, keepdims=True),
                jnp.max(new_scores, axis=1, keepdims=True),
            )
            shares = jnp.exp2((scores - top) * COEF)
            new_shares = jnp.exp2((new_scores - top) * COEF)
            summed = jnp.sum(shares, axis=1, keepdims=True) + jnp.sum(
                new_shares, axis=1, keepdims=True
            )
            hs_v[j] = shares.astype(BF16)
            hn_v[j] = new_shares.astype(BF16)
            sums.append(summed)
            total = jnp.where(lane == r, top * COEF + jnp.log2(summed), total)
            between(j)
        hl_c[0:rows] = total
        home[c][1].wait()
        for j in range(per_chunk):
            r = c * per_chunk + j
            both = nn(hs_v[j], hv_v[r])
            out = jnp.concatenate([both[:part_rows, :HD], both[part_rows:, HD:]], axis=0)
            out = out + nn(hn_v[j], nv_v[...])
            ho_v[r] = (out / sums[j]).astype(BF16)

    def nothing(j):
        pass

    home_part(0, nothing)
    home_part(1, nothing)

    all_of(0, tab_r).wait_recv()

    picks = {d: jnp.maximum(tab_r[pool_peer(d), 0, 0], 0) for d in FAR_FIRST}
    mine = jnp.maximum(tab_r[me, 0, 0], 0)
    halves = [slice(0, part_rows), slice(part_rows, rows)]

    def send_query(k, d):
        peer = pool_peer(d)
        qs[k][peer] = q_v[picks[d], halves[k]]
        remote(1 + k, qs[k].at[peer], qr[k].at[me], d).start()

    for k in range(2):
        qr[k][me] = q_v[mine, halves[k]]
    for d in FAR_FIRST:
        send_query(0, d)
    for copy in weights:
        copy.start()

    def query_sends(j):
        for d in FAR_FIRST[j * 8 : j * 8 + 8]:
            send_query(1, d)

    home_part(2, query_sends)
    home_part(3, nothing)
    for d in range(n):
        inv_s[d] = inv_v[pool_peer(d), 0, 0]

    small[3].wait()
    small[4].wait()
    part_lane = iota((part_rows, 128), 1)

    def send_result(k, d):
        peer = pool_peer(d)
        rs[k][peer] = res_v[inv_s[d], halves[k]]
        remote(4 + k, rs[k].at[peer], rr[k].at[me], d).start()

    def send_lse(d):
        remote(3, ls_v.at[pool_peer(d)], lr_v.at[me], d).start()

    for k in range(2):
        all_of(1 + k, qr[k]).wait_recv()
        width = slice(k * HD, k * HD + HD)
        total = jnp.zeros((part_rows, 128), F32)
        sums = []
        for l in range(slots):
            owner = lreq[l] // reqs
            shares, summed, lse = head_shares(qr[k][owner], pk_v[l, :, width], lblk[l] * BLOCK)
            sh_v[l] = shares
            sums.append(summed)
            total = jnp.where(part_lane == owner, lse, total)
        pl_c[halves[k]] = total
        if k == 1:
            ls_v[...] = pl_c[...].T[0:n].reshape(n, 1, 128)
            lr_v[me] = ls_v[me]
        for l in range(slots):
            out = nn(sh_v[l], pv_v[l, :, width])
            res_v[l, halves[k]] = (out / sums[l]).astype(BF16)
            if k == 1:
                for d in FAR_FIRST[2 * l : 2 * l + 2]:
                    send_lse(d)
        rr[k][me] = res_v[inv_s[0], halves[k]]
        if k == 0:
            for d in FAR_FIRST:
                send_result(0, d)
    eight = iota((8, 128), 1) // 16 == iota((8, 128), 0)
    local = tab_r[...].reshape(n, 128)
    parts = n + reqs
    seg = jnp.concatenate([local, iota((reqs, 128), 0)], axis=0)
    seg_lane = jnp.concatenate(
        [
            jnp.sum(jnp.where(eight, seg[c * 8 : c * 8 + 8], 0), axis=0, keepdims=True)
            for c in range(parts // 8)
        ],
        axis=1,
    )
    block = (16, parts * 16)
    b_row, b_col = iota(block, 0), iota(block, 1)
    head_step = b_col % 16 - b_row % steps
    owner_row = seg_lane - b_row // steps
    for i in range(16):
        same = (head_step == i // 4 * steps) & (owner_row == i % 4 * 4)
        e_v[i] = jnp.where(same, 1.0, 0.0).astype(BF16)
        for d in FAR_FIRST[2 * i : 2 * i + 2]:
            send_result(1, d)
    all_of(3, lr_v).wait_recv()
    lse = jnp.concatenate([lr_v[...].reshape(n, 128), hl_c[...].T[0:reqs]], axis=0)
    big = lse
    for r in range(reqs):
        hit = seg == r
        big = jnp.where(hit, jnp.max(jnp.where(hit, lse, MASKED), axis=0, keepdims=True), big)
    share = jnp.where(seg >= 0, jnp.exp2(lse - big), 0.0)
    total = jnp.ones_like(share)
    for r in range(reqs):
        hit = seg == r
        total = jnp.where(
            hit, jnp.sum(jnp.where(hit, share, 0.0), axis=0, keepdims=True), total
        )
    spread = nn((share / total).astype(BF16), t_v[...])

    def build(g):
        wide = g * 128
        along = jnp.concatenate(
            [
                jnp.sum(
                    jnp.where(eight, spread[c * 8 : c * 8 + 8, wide : wide + 128], 0.0),
                    axis=0,
                    keepdims=True,
                )
                for c in range(parts // 8)
            ],
            axis=1,
        )
        along = jnp.broadcast_to(along, block).astype(BF16)
        return (e_v[...] * along[None]).reshape(256, parts * 16)

    def merge(k, a_v, lefts):
        all_of(4 + k, rr[k]).wait_recv()
        for g in range(part_rows // 16):
            group = slice(g * 16, g * 16 + 16)
            own = slice(k * part_rows + g * 16, k * part_rows + g * 16 + 16)
            right = jnp.concatenate(
                [rr[k][:, group].reshape(n * 16, HD), ho_v[:, own].reshape(reqs * 16, HD)],
                axis=0,
            )
            merged = nn(lefts(g), right).astype(BF16)
            for h in range(4):
                head = g * 4 + h
                a_v[:, head * HD : head * HD + HD] = merged[h * rows : h * rows + rows]

    for g in range(2):
        l_v[g] = build(2 + g)
    merge(0, a0_v, build)
    for i in range(t):
        weights[i].wait()
        acc_v[i] = nn(a0_v[...], w_v[i, 0:deep])
    merge(1, a1_v, lambda g: l_v[g])

    half = cols // 2
    left, right = slice(0, half), slice(half, cols)

    def projected(i, at):
        return acc_v[i, :, at] + nn(a1_v[...], w_v[i, deep : 2 * deep, at])

    def to_neighbour(i, src, side):
        return pltpu.make_async_remote_copy(
            src_ref=src,
            dst_ref=pr_v.at[i],
            send_sem=rsend_sem.at[i],
            recv_sem=rrecv_sem.at[i],
            device_id={"tp": tp_peer(side)},
            device_id_type=MESH,
        )

    up, down = 1, t - 1
    ring = [
        to_neighbour(i, ps_v.at[i], side)
        for i, side in enumerate([up, down, up, down, up, down])
    ]
    def send(i, value):
        ps_v[i] = value.astype(BF16)
        ring[i].start()

    send(0, projected(0, left))
    send(1, projected(0, right))
    send(2, projected(1, right))
    send(3, projected(2, left))
    above = projected(1, left)
    ring[0].wait_recv()
    send(4, above + pr_v[0].astype(F32))
    below = projected(2, right)
    ring[1].wait_recv()
    send(5, below + pr_v[1].astype(F32))
    own = jnp.concatenate([projected(3, left), projected(3, right)], axis=1)
    for i in range(2, 6):
        ring[i].wait_recv()
    from_below = jnp.concatenate([pr_v[4], pr_v[2]], axis=1).astype(F32)
    from_above = jnp.concatenate([pr_v[3], pr_v[5]], axis=1).astype(F32)
    result = own + from_below + from_above

    first = iota((8, 8, HD), 1) < 4
    for g in range(2):
        even, odd = [], []
        for k in range(2):
            c = (g * 2 + k) * 2 * HD
            left = result[:, c : c + HD].reshape(8, 8, HD)
            right = result[:, c + HD : c + 2 * HD].reshape(8, 8, HD)
            even.append(jnp.where(first, left, pltpu.roll(right, 4, 1)))
            odd.append(jnp.where(first, pltpu.roll(left, 4, 1), right))
        for k, both in enumerate([even, odd]):
            out_ref[:, k, g * 16 : g * 16 + 16] = jnp.concatenate(both, axis=1).astype(BF16)

    all_of(0, tab_s).wait_send()
    for k in range(2):
        all_of(1 + k, qs[k]).wait_send()
        all_of(4 + k, rs[k]).wait_send()
    all_of(3, ls_v).wait_send()
    for copy in ring:
        copy.wait_send()


def per_device(
    queries, home_keys, home_values, new_keys, new_values, home_len,
    piece_keys, piece_values, lend_request, lend_blocks, out_weight,
):
    n = lax.axis_size("pool")
    t = lax.axis_size("tp")
    reqs, steps, features = queries.shape
    heads = features // HD
    kv = new_keys.shape[2] // HD
    rows = heads * steps
    slots, piece = piece_keys.shape[:2]
    cols = out_weight.shape[1] // t

    def head_rows(x):
        count = x.shape[2] // HD
        return x.reshape(reqs, steps, count, HD).transpose(0, 2, 1, 3)

    q = head_rows(queries).reshape(reqs, rows, HD)
    nk = head_rows(new_keys).reshape(reqs * kv * steps, HD)
    nv = head_rows(new_values).reshape(reqs * kv * steps, HD)
    hbm = pl.BlockSpec(memory_space=pl.ANY)
    chunks = 4
    vmem = pltpu.VMEM
    out = pl.pallas_call(
        functools.partial(kernel, n, t),
        out_shape=vmem((reqs // 2, 2, cols // HD * steps, HD), BF16),
        in_specs=[hbm] * 11,
        out_specs=pl.BlockSpec(memory_space=pltpu.VMEM),
        scratch_shapes=[
            *[pltpu.SMEM((reqs,), jnp.int32)] * 3,
            vmem(q.shape, BF16),
            vmem(nk.shape, BF16),
            vmem(nv.shape, BF16),
            vmem(home_keys.shape, BF16),
            vmem(home_values.shape, BF16),
            vmem(piece_keys.shape, BF16),
            vmem(piece_values.shape, BF16),
            vmem((t, features, cols), BF16),
            vmem((reqs, rows, 128), F32),
            vmem((n, 1, 128), jnp.int32),
            vmem((n, 1, 128), jnp.int32),
            vmem((n, 1, 128), jnp.int32),
            pltpu.SMEM((n,), jnp.int32),
            *[vmem((n, rows // 2, HD), BF16)] * 4,
            vmem((slots, rows, HD), BF16),
            vmem((slots, rows // 2, piece), BF16),
            *[vmem((n, rows // 2, HD), BF16)] * 4,
            *[vmem((n, 1, 128), F32)] * 2,
            vmem((reqs, rows, HD), BF16),
            vmem((reqs // chunks, rows, home_keys.shape[1]), BF16),
            vmem((reqs // chunks, rows, 128), BF16),
            *[vmem((128, 128), F32)] * 2,
            vmem((16, 16, (n + reqs) * 16), BF16),
            vmem((128, (rows // 16) * 128), BF16),
            vmem((2, 256, (n + reqs) * 16), BF16),
            *[vmem((reqs * steps, features // 2), BF16)] * 2,
            vmem((t, reqs * steps, cols), F32),
            vmem((6, reqs * steps, cols // 2), BF16),
            vmem((6, reqs * steps, cols // 2), BF16),
            pltpu.SemaphoreType.DMA((8,)),
            pltpu.SemaphoreType.DMA((2, chunks)),
            pltpu.SemaphoreType.DMA((t,)),
            pltpu.SemaphoreType.DMA((6,)),
            pltpu.SemaphoreType.DMA((6,)),
            pltpu.SemaphoreType.DMA((6,)),
            pltpu.SemaphoreType.DMA((6,)),
        ],
        compiler_params=pltpu.CompilerParams(
            collective_id=0, has_side_effects=True, vmem_limit_bytes=56 * 1024 * 1024
        ),
        name="lent_attention",
    )(
        home_len, lend_request, lend_blocks, q, nk, nv,
        home_keys, home_values, piece_keys, piece_values, out_weight,
    )
    out = out.reshape(reqs, cols // HD, steps, HD).transpose(0, 2, 1, 3)
    return out.reshape(reqs, steps, cols)


def solution(mesh):
    placed = (
        P("pool", None, "tp"),
        P("pool", None, "tp"),
        P("pool", None, "tp"),
        P("pool", None, "tp"),
        P("pool", None, "tp"),
        P("pool"),
        P("pool", None, "tp"),
        P("pool", None, "tp"),
        P("pool"),
        P("pool"),
        P("tp", None),
    )
    return jax.shard_map(
        per_device, mesh=mesh, in_specs=placed, out_specs=P("pool", None, "tp"), check_vma=False
    )
```

```python
import functools
import math

import jax
import jax.numpy as jnp
from jax import lax
from jax.experimental import pallas as pl
from jax.experimental.pallas import tpu as pltpu
from jax.sharding import PartitionSpec as P

QH = 64
KVH = 8
HD = 128
BLOCK = 128
MASKED = -1e30
MESH = pl.DeviceIdType.MESH
F32 = jnp.float32
BF16 = jnp.bfloat16
COEF = math.log2(math.e) / math.sqrt(HD)


def hops(d):
    dy, dx = d // 8, d // 2 % 4
    return min(dy, 4 - dy) + min(dx, 4 - dx)


FAR_FIRST = sorted(range(1, 32), key=lambda d: -hops(d))


def nt(a, b):
    return lax.dot_general(a, b, (((1,), (1,)), ((), ())), preferred_element_type=F32)


def nn(a, b):
    return lax.dot_general(a, b, (((1,), (0,)), ((), ())), preferred_element_type=F32)


def iota(shape, dim):
    return lax.broadcasted_iota(jnp.int32, shape, dim)


def wide_query(q):
    half = q.shape[0] // 2
    zero = jnp.zeros((half, HD), BF16)
    return jnp.concatenate(
        [
            jnp.concatenate([q[:half], zero], axis=1),
            jnp.concatenate([zero, q[half:]], axis=1),
        ],
        axis=0,
    )


def head_shares(q, keys, valid_len):
    scores = nt(q, keys)
    scores = jnp.where(iota(scores.shape, 1) < valid_len, scores, MASKED)
    top = jnp.max(scores, axis=1, keepdims=True)
    shares = jnp.exp2((scores - top) * COEF)
    summed = jnp.sum(shares, axis=1, keepdims=True)
    return shares.astype(BF16), summed, top * COEF + jnp.log2(summed)


def kernel(
    n, t,
    hlen_h, lreq_h, lblk_h, q_h, nk_h, nv_h, hk_h, hv_h, pk_h, pv_h, w_h,
    out_ref,
    hlen, lreq, lblk, q_v, nk_v, nv_v, hk_v, hv_v, pk_v, pv_v, w_v,
    sn_v, tab_s, tab_r, inv_v, inv_s,
    qs0_v, qs1_v, qr0_v, qr1_v, res_v, sh_v, rs0_v, rs1_v, rr0_v, rr1_v, ls_v, lr_v,
    ho_v, hs_v, hn_v, hl_c, pl_c, e_v, t_v, l_v, a0_v, a1_v, acc_v, ps_v, pr_v,
    in_sem, home_sem, w_sem, send_sem, recv_sem, rsend_sem, rrecv_sem,
):
    me = lax.axis_index("pool")
    tp = lax.axis_index("tp")
    reqs, rows, _ = q_v.shape
    slots = pk_v.shape[0]
    steps = 4
    home_chunks = home_sem.shape[1]
    per_chunk = reqs // home_chunks
    cols = w_v.shape[2]
    part_rows = rows // 2
    deep = a0_v.shape[1]
    qs, qr = (qs0_v, qs1_v), (qr0_v, qr1_v)
    rs, rr = (rs0_v, rs1_v), (rr0_v, rr1_v)

    def pool_peer(d):
        return jnp.where(me + d >= n, me + d - n, me + d)

    def tp_peer(d):
        return lax.rem(tp + d, t)

    barrier = pltpu.get_barrier_semaphore()

    for d in range(1, t):
        pl.semaphore_signal(
            barrier, inc=1, device_id={"tp": tp_peer(d)}, device_id_type=MESH
        )
    for d in FAR_FIRST:
        pl.semaphore_signal(
            barrier, inc=1, device_id={"pool": pool_peer(d)}, device_id_type=MESH
        )

    small = [
        pltpu.make_async_copy(src, dst, in_sem.at[i])
        for i, (src, dst) in enumerate(
            [
                (q_h, q_v), (nk_h, nk_v), (nv_h, nv_v), (pk_h, pk_v), (pv_h, pv_v),
                (lreq_h, lreq), (hlen_h, hlen), (lblk_h, lblk),
            ]
        )
    ]
    for i in (5, 6, 7, 0, 1, 2):
        small[i].start()
    home = []
    for c in range(home_chunks):
        part = pl.ds(c * per_chunk, per_chunk)
        home.append(
            [
                pltpu.make_async_copy(hk_h.at[part], hk_v.at[part], home_sem.at[0, c]),
                pltpu.make_async_copy(hv_h.at[part], hv_v.at[part], home_sem.at[1, c]),
            ]
        )
    for c in range(home_chunks):
        home[c][0].start()
        home[c][1].start()
    small[3].start()
    small[4].start()
    order = [2, 1, 3, 0]
    weights = []
    for i, d in enumerate(order):
        column = pl.multiple_of(tp_peer(d) * cols, cols)
        weights.append(
            pltpu.make_async_copy(w_h.at[:, pl.ds(column, cols)], w_v.at[i], w_sem.at[i])
        )

    for i in (5, 6, 7):
        small[i].wait()
    owner_id = iota((n, 128), 0)
    wanted = jnp.full((n, 128), -1, jnp.int32)
    slot_of = jnp.zeros((n, 128), jnp.int32)
    for l in range(slots):
        request = lreq[l]
        owner = request // reqs
        hit = owner_id == owner
        wanted = jnp.where(hit, request - owner * reqs, wanted)
        slot_of = jnp.where(hit, l, slot_of)
    tab_s[...] = wanted.reshape(n, 1, 128)
    inv_v[...] = slot_of.reshape(n, 1, 128)

    def remote(phase, src, dst, d):
        return pltpu.make_async_remote_copy(
            src_ref=src,
            dst_ref=dst,
            send_sem=send_sem.at[phase],
            recv_sem=recv_sem.at[phase],
            device_id={"pool": pool_peer(d)},
            device_id_type=MESH,
        )

    def all_of(phase, buffer):
        part = buffer.at[pl.ds(0, n - 1)]
        return remote(phase, part, part, 1)

    pl.semaphore_wait(barrier, n - 1 + t - 1)

    for d in FAR_FIRST:
        remote(0, tab_s.at[pool_peer(d)], tab_r.at[me], d).start()
    tab_r[me] = tab_s[me]
    for copy in weights:
        copy.start()

    for copy in small[:3]:
        copy.wait()
    sn_v[...] = nt(q_v[...].reshape(reqs * rows, HD), nk_v[...]).reshape(reqs, rows, HD)
    hl_c[...] = jnp.zeros(hl_c.shape, F32)
    pl_c[...] = jnp.zeros(pl_c.shape, F32)
    lane = iota((rows, 128), 1)
    row = iota((rows, 128), 0)

    def home_part(c, between):
        home[c][0].wait()
        total = hl_c[0:rows]
        sums = []
        for j in range(per_chunk):
            r = c * per_chunk + j
            low = r * (2 * steps) + (row // (rows // 2)) * steps
            seen = (lane >= low) & (lane <= low + row % steps)
            new_scores = jnp.where(seen, sn_v[r], MASKED)
            scores = nt(wide_query(q_v[r]), hk_v[r])
            scores = jnp.where(iota(scores.shape, 1) < hlen[r], scores, MASKED)
            top = jnp.maximum(
                jnp.max(scores, axis=1, keepdims=True),
                jnp.max(new_scores, axis=1, keepdims=True),
            )
            shares = jnp.exp2((scores - top) * COEF)
            new_shares = jnp.exp2((new_scores - top) * COEF)
            summed = jnp.sum(shares, axis=1, keepdims=True) + jnp.sum(
                new_shares, axis=1, keepdims=True
            )
            hs_v[j] = shares.astype(BF16)
            hn_v[j] = new_shares.astype(BF16)
            sums.append(summed)
            total = jnp.where(lane == r, top * COEF + jnp.log2(summed), total)
            between(j)
        hl_c[0:rows] = total
        home[c][1].wait()
        for j in range(per_chunk):
            r = c * per_chunk + j
            both = nn(hs_v[j], hv_v[r])
            out = jnp.concatenate([both[:part_rows, :HD], both[part_rows:, HD:]], axis=0)
            out = out + nn(hn_v[j], nv_v[...])
            ho_v[r] = (out / sums[j]).astype(BF16)

    def nothing(j):
        pass

    home_part(0, nothing)

    all_of(0, tab_r).wait_recv()

    picks = {d: jnp.maximum(tab_r[pool_peer(d), 0, 0], 0) for d in FAR_FIRST}
    mine = jnp.maximum(tab_r[me, 0, 0], 0)
    halves = [slice(0, part_rows), slice(part_rows, rows)]

    def send_query(k, d):
        peer = pool_peer(d)
        qs[k][peer] = q_v[picks[d], halves[k]]
        remote(1 + k, qs[k].at[peer], qr[k].at[me], d).start()

    for k in range(2):
        qr[k][me] = q_v[mine, halves[k]]
    for d in FAR_FIRST:
        send_query(0, d)

    def query_sends(j):
        for d in FAR_FIRST[j * 8 : j * 8 + 8]:
            send_query(1, d)

    home_part(1, query_sends)
    home_part(2, nothing)
    home_part(3, nothing)
    t_row = iota(t_v.shape, 0)
    t_col = iota(t_v.shape, 1)
    t_v[...] = jnp.where(
        t_row == (t_col // 128) * 16 + t_col % 16, 1.0, 0.0
    ).astype(BF16)
    for d in range(n):
        inv_s[d] = inv_v[pool_peer(d), 0, 0]

    small[3].wait()
    small[4].wait()
    part_lane = iota((part_rows, 128), 1)

    def send_result(k, d):
        peer = pool_peer(d)
        rs[k][peer] = res_v[inv_s[d], halves[k]]
        remote(4 + k, rs[k].at[peer], rr[k].at[me], d).start()

    def send_lse(d):
        remote(3, ls_v.at[pool_peer(d)], lr_v.at[me], d).start()

    for k in range(2):
        all_of(1 + k, qr[k]).wait_recv()
        width = slice(k * HD, k * HD + HD)
        total = jnp.zeros((part_rows, 128), F32)
        sums = []
        for l in range(slots):
            owner = lreq[l] // reqs
            shares, summed, lse = head_shares(qr[k][owner], pk_v[l, :, width], lblk[l] * BLOCK)
            sh_v[l] = shares
            sums.append(summed)
            total = jnp.where(part_lane == owner, lse, total)
        pl_c[halves[k]] = total
        if k == 1:
            ls_v[...] = pl_c[...].T[0:n].reshape(n, 1, 128)
            lr_v[me] = ls_v[me]
        for l in range(slots):
            out = nn(sh_v[l], pv_v[l, :, width])
            res_v[l, halves[k]] = (out / sums[l]).astype(BF16)
            if k == 1:
                for d in FAR_FIRST[2 * l : 2 * l + 2]:
                    send_lse(d)
        rr[k][me] = res_v[inv_s[0], halves[k]]
        if k == 0:
            for d in FAR_FIRST:
                send_result(0, d)
    eight = iota((8, 128), 1) // 16 == iota((8, 128), 0)
    local = tab_r[...].reshape(n, 128)
    parts = n + reqs
    seg = jnp.concatenate([local, iota((reqs, 128), 0)], axis=0)
    seg_lane = jnp.concatenate(
        [
            jnp.sum(jnp.where(eight, seg[c * 8 : c * 8 + 8], 0), axis=0, keepdims=True)
            for c in range(parts // 8)
        ],
        axis=1,
    )
    block = (16, parts * 16)
    b_row, b_col = iota(block, 0), iota(block, 1)
    head_step = b_col % 16 - b_row % steps
    owner_row = seg_lane - b_row // steps
    for i in range(16):
        same = (head_step == i // 4 * steps) & (owner_row == i % 4 * 4)
        e_v[i] = jnp.where(same, 1.0, 0.0).astype(BF16)
        for d in FAR_FIRST[2 * i : 2 * i + 2]:
            send_result(1, d)
    all_of(3, lr_v).wait_recv()
    lse = jnp.concatenate([lr_v[...].reshape(n, 128), hl_c[...].T[0:reqs]], axis=0)
    big = lse
    for r in range(reqs):
        hit = seg == r
        big = jnp.where(hit, jnp.max(jnp.where(hit, lse, MASKED), axis=0, keepdims=True), big)
    share = jnp.where(seg >= 0, jnp.exp2(lse - big), 0.0)
    total = jnp.ones_like(share)
    for r in range(reqs):
        hit = seg == r
        total = jnp.where(
            hit, jnp.sum(jnp.where(hit, share, 0.0), axis=0, keepdims=True), total
        )
    spread = nn((share / total).astype(BF16), t_v[...])

    def build(g):
        wide = g * 128
        along = jnp.concatenate(
            [
                jnp.sum(
                    jnp.where(eight, spread[c * 8 : c * 8 + 8, wide : wide + 128], 0.0),
                    axis=0,
                    keepdims=True,
                )
                for c in range(parts // 8)
            ],
            axis=1,
        )
        along = jnp.broadcast_to(along, block).astype(BF16)
        return (e_v[...] * along[None]).reshape(256, parts * 16)

    def merge(k, a_v, lefts):
        all_of(4 + k, rr[k]).wait_recv()
        for g in range(part_rows // 16):
            group = slice(g * 16, g * 16 + 16)
            own = slice(k * part_rows + g * 16, k * part_rows + g * 16 + 16)
            right = jnp.concatenate(
                [rr[k][:, group].reshape(n * 16, HD), ho_v[:, own].reshape(reqs * 16, HD)],
                axis=0,
            )
            merged = nn(lefts(g), right).astype(BF16)
            for h in range(4):
                head = g * 4 + h
                a_v[:, head * HD : head * HD + HD] = merged[h * rows : h * rows + rows]

    for g in range(2):
        l_v[g] = build(2 + g)
    merge(0, a0_v, build)
    for i in range(t):
        weights[i].wait()
        acc_v[i] = nn(a0_v[...], w_v[i, 0:deep])
    merge(1, a1_v, lambda g: l_v[g])

    half = cols // 2
    left, right = slice(0, half), slice(half, cols)

    def projected(i, at):
        return acc_v[i, :, at] + nn(a1_v[...], w_v[i, deep : 2 * deep, at])

    def to_neighbour(i, src, side):
        return pltpu.make_async_remote_copy(
            src_ref=src,
            dst_ref=pr_v.at[i],
            send_sem=rsend_sem.at[i],
            recv_sem=rrecv_sem.at[i],
            device_id={"tp": tp_peer(side)},
            device_id_type=MESH,
        )

    up, down = 1, t - 1
    ring = [
        to_neighbour(i, ps_v.at[i], side)
        for i, side in enumerate([up, down, up, down, up, down])
    ]
    def send(i, value):
        ps_v[i] = value.astype(BF16)
        ring[i].start()

    send(0, projected(0, left))
    send(1, projected(0, right))
    send(2, projected(1, right))
    send(3, projected(2, left))
    above = projected(1, left)
    ring[0].wait_recv()
    send(4, above + pr_v[0].astype(F32))
    below = projected(2, right)
    ring[1].wait_recv()
    send(5, below + pr_v[1].astype(F32))
    own = jnp.concatenate([projected(3, left), projected(3, right)], axis=1)
    for i in range(2, 6):
        ring[i].wait_recv()
    from_below = jnp.concatenate([pr_v[4], pr_v[2]], axis=1).astype(F32)
    from_above = jnp.concatenate([pr_v[3], pr_v[5]], axis=1).astype(F32)
    result = own + from_below + from_above

    first = iota((8, 8, HD), 1) < 4
    for g in range(2):
        even, odd = [], []
        for k in range(2):
            c = (g * 2 + k) * 2 * HD
            left = result[:, c : c + HD].reshape(8, 8, HD)
            right = result[:, c + HD : c + 2 * HD].reshape(8, 8, HD)
            even.append(jnp.where(first, left, pltpu.roll(right, 4, 1)))
            odd.append(jnp.where(first, pltpu.roll(left, 4, 1), right))
        for k, both in enumerate([even, odd]):
            out_ref[:, k, g * 16 : g * 16 + 16] = jnp.concatenate(both, axis=1).astype(BF16)

    all_of(0, tab_s).wait_send()
    for k in range(2):
        all_of(1 + k, qs[k]).wait_send()
        all_of(4 + k, rs[k]).wait_send()
    all_of(3, ls_v).wait_send()
    for copy in ring:
        copy.wait_send()


def per_device(
    queries, home_keys, home_values, new_keys, new_values, home_len,
    piece_keys, piece_values, lend_request, lend_blocks, out_weight,
):
    n = lax.axis_size("pool")
    t = lax.axis_size("tp")
    reqs, steps, features = queries.shape
    heads = features // HD
    kv = new_keys.shape[2] // HD
    rows = heads * steps
    slots, piece = piece_keys.shape[:2]
    cols = out_weight.shape[1] // t

    def head_rows(x):
        count = x.shape[2] // HD
        return x.reshape(reqs, steps, count, HD).transpose(0, 2, 1, 3)

    q = head_rows(queries).reshape(reqs, rows, HD)
    nk = head_rows(new_keys).reshape(reqs * kv * steps, HD)
    nv = head_rows(new_values).reshape(reqs * kv * steps, HD)
    hbm = pl.BlockSpec(memory_space=pl.ANY)
    chunks = 4
    vmem = pltpu.VMEM
    out = pl.pallas_call(
        functools.partial(kernel, n, t),
        out_shape=vmem((reqs // 2, 2, cols // HD * steps, HD), BF16),
        in_specs=[hbm] * 11,
        out_specs=pl.BlockSpec(memory_space=pltpu.VMEM),
        scratch_shapes=[
            *[pltpu.SMEM((reqs,), jnp.int32)] * 3,
            vmem(q.shape, BF16),
            vmem(nk.shape, BF16),
            vmem(nv.shape, BF16),
            vmem(home_keys.shape, BF16),
            vmem(home_values.shape, BF16),
            vmem(piece_keys.shape, BF16),
            vmem(piece_values.shape, BF16),
            vmem((t, features, cols), BF16),
            vmem((reqs, rows, 128), F32),
            vmem((n, 1, 128), jnp.int32),
            vmem((n, 1, 128), jnp.int32),
            vmem((n, 1, 128), jnp.int32),
            pltpu.SMEM((n,), jnp.int32),
            *[vmem((n, rows // 2, HD), BF16)] * 4,
            vmem((slots, rows, HD), BF16),
            vmem((slots, rows // 2, piece), BF16),
            *[vmem((n, rows // 2, HD), BF16)] * 4,
            *[vmem((n, 1, 128), F32)] * 2,
            vmem((reqs, rows, HD), BF16),
            vmem((reqs // chunks, rows, home_keys.shape[1]), BF16),
            vmem((reqs // chunks, rows, 128), BF16),
            *[vmem((128, 128), F32)] * 2,
            vmem((16, 16, (n + reqs) * 16), BF16),
            vmem((128, (rows // 16) * 128), BF16),
            vmem((2, 256, (n + reqs) * 16), BF16),
            *[vmem((reqs * steps, features // 2), BF16)] * 2,
            vmem((t, reqs * steps, cols), F32),
            vmem((6, reqs * steps, cols // 2), BF16),
            vmem((6, reqs * steps, cols // 2), BF16),
            pltpu.SemaphoreType.DMA((8,)),
            pltpu.SemaphoreType.DMA((2, chunks)),
            pltpu.SemaphoreType.DMA((t,)),
            pltpu.SemaphoreType.DMA((6,)),
            pltpu.SemaphoreType.DMA((6,)),
            pltpu.SemaphoreType.DMA((6,)),
            pltpu.SemaphoreType.DMA((6,)),
        ],
        compiler_params=pltpu.CompilerParams(
            collective_id=0, has_side_effects=True, vmem_limit_bytes=56 * 1024 * 1024
        ),
        name="lent_attention",
    )(
        home_len, lend_request, lend_blocks, q, nk, nv,
        home_keys, home_values, piece_keys, piece_values, out_weight,
    )
    out = out.reshape(reqs, cols // HD, steps, HD).transpose(0, 2, 1, 3)
    return out.reshape(reqs, steps, cols)


def solution(mesh):
    placed = (
        P("pool", None, "tp"),
        P("pool", None, "tp"),
        P("pool", None, "tp"),
        P("pool", None, "tp"),
        P("pool", None, "tp"),
        P("pool"),
        P("pool", None, "tp"),
        P("pool", None, "tp"),
        P("pool"),
        P("pool"),
        P("tp", None),
    )
    return jax.shard_map(
        per_device, mesh=mesh, in_specs=placed, out_specs=P("pool", None, "tp"), check_vma=False
    )
```

```python
import functools
import math

import jax
import jax.numpy as jnp
from jax import lax
from jax.experimental import pallas as pl
from jax.experimental.pallas import tpu as pltpu
from jax.sharding import PartitionSpec as P

QH = 64
KVH = 8
HD = 128
BLOCK = 128
MASKED = -1e30
MESH = pl.DeviceIdType.MESH
F32 = jnp.float32
BF16 = jnp.bfloat16
COEF = math.log2(math.e) / math.sqrt(HD)


def hops(d):
    dy, dx = d // 8, d // 2 % 4
    return min(dy, 4 - dy) + min(dx, 4 - dx)


FAR_FIRST = sorted(range(1, 32), key=lambda d: -hops(d))


def nt(a, b):
    return lax.dot_general(a, b, (((1,), (1,)), ((), ())), preferred_element_type=F32)


def nn(a, b):
    return lax.dot_general(a, b, (((1,), (0,)), ((), ())), preferred_element_type=F32)


def iota(shape, dim):
    return lax.broadcasted_iota(jnp.int32, shape, dim)


def wide_query(q):
    half = q.shape[0] // 2
    zero = jnp.zeros((half, HD), BF16)
    return jnp.concatenate(
        [
            jnp.concatenate([q[:half], zero], axis=1),
            jnp.concatenate([zero, q[half:]], axis=1),
        ],
        axis=0,
    )


def head_shares(q, keys, valid_len):
    scores = nt(q, keys)
    scores = jnp.where(iota(scores.shape, 1) < valid_len, scores, MASKED)
    top = jnp.max(scores, axis=1, keepdims=True)
    shares = jnp.exp2((scores - top) * COEF)
    summed = jnp.sum(shares, axis=1, keepdims=True)
    return shares.astype(BF16), summed, top * COEF + jnp.log2(summed)


def kernel(
    n, t,
    hlen_h, lreq_h, lblk_h, q_h, nk_h, nv_h, hk_h, hv_h, pk_h, pv_h, w_h,
    out_ref,
    hlen, lreq, lblk, q_v, nk_v, nv_v, hk_v, hv_v, pk_v, pv_v, w_v,
    sn_v, tab_s, tab_r, inv_v, inv_s,
    qs0_v, qs1_v, qr0_v, qr1_v, res_v, sh_v, rs0_v, rs1_v, rr0_v, rr1_v, ls_v, lr_v,
    ho_v, hs_v, hn_v, hl_c, pl_c, e_v, t_v, l_v, a0_v, a1_v, acc_v, ps_v, pr_v,
    in_sem, home_sem, w_sem, send_sem, recv_sem, rsend_sem, rrecv_sem,
):
    me = lax.axis_index("pool")
    tp = lax.axis_index("tp")
    reqs, rows, _ = q_v.shape
    slots = pk_v.shape[0]
    steps = 4
    home_chunks = home_sem.shape[1]
    per_chunk = reqs // home_chunks
    cols = w_v.shape[2]
    part_rows = rows // 2
    deep = a0_v.shape[1]
    qs, qr = (qs0_v, qs1_v), (qr0_v, qr1_v)
    rs, rr = (rs0_v, rs1_v), (rr0_v, rr1_v)

    peers = {d: jnp.where(me + d >= n, me + d - n, me + d) for d in range(n)}

    def pool_peer(d):
        return peers[d]

    def tp_peer(d):
        return lax.rem(tp + d, t)

    barrier = pltpu.get_barrier_semaphore()

    for d in range(1, t):
        pl.semaphore_signal(
            barrier, inc=1, device_id={"tp": tp_peer(d), "pool": me}, device_id_type=MESH
        )
    for d in FAR_FIRST:
        pl.semaphore_signal(
            barrier, inc=1, device_id={"tp": tp, "pool": pool_peer(d)}, device_id_type=MESH
        )

    small = [
        pltpu.make_async_copy(src, dst, in_sem.at[i])
        for i, (src, dst) in enumerate(
            [
                (q_h, q_v), (nk_h, nk_v), (nv_h, nv_v), (pk_h, pk_v), (pv_h, pv_v),
                (lreq_h, lreq), (hlen_h, hlen), (lblk_h, lblk),
            ]
        )
    ]
    for i in (5, 6, 7, 0, 1, 2):
        small[i].start()
    home = []
    for c in range(home_chunks):
        part = pl.ds(c * per_chunk, per_chunk)
        home.append(
            [
                pltpu.make_async_copy(hk_h.at[part], hk_v.at[part], home_sem.at[0, c]),
                pltpu.make_async_copy(hv_h.at[part], hv_v.at[part], home_sem.at[1, c]),
            ]
        )
    for c in range(home_chunks):
        home[c][0].start()
        home[c][1].start()
    small[3].start()
    small[4].start()
    order = [2, 1, 3, 0]
    weights = []
    for i, d in enumerate(order):
        column = pl.multiple_of(tp_peer(d) * cols, cols)
        weights.append(
            pltpu.make_async_copy(w_h.at[:, pl.ds(column, cols)], w_v.at[i], w_sem.at[i])
        )

    for i in (5, 6, 7):
        small[i].wait()
    owner_id = iota((n, 128), 0)
    wanted = jnp.full((n, 128), -1, jnp.int32)
    slot_of = jnp.zeros((n, 128), jnp.int32)
    for l in range(slots):
        request = lreq[l]
        owner = request // reqs
        hit = owner_id == owner
        wanted = jnp.where(hit, request - owner * reqs, wanted)
        slot_of = jnp.where(hit, l, slot_of)
    tab_s[...] = wanted.reshape(n, 1, 128)
    inv_v[...] = slot_of.reshape(n, 1, 128)

    def remote(phase, src, dst, d):
        return pltpu.make_async_remote_copy(
            src_ref=src,
            dst_ref=dst,
            send_sem=send_sem.at[phase],
            recv_sem=recv_sem.at[phase],
            device_id={"tp": tp, "pool": pool_peer(d)},
            device_id_type=MESH,
        )

    def all_of(phase, buffer):
        part = buffer.at[pl.ds(0, n - 1)]
        return remote(phase, part, part, 1)

    pl.semaphore_wait(barrier, n - 1 + t - 1)

    for d in FAR_FIRST:
        remote(0, tab_s.at[pool_peer(d)], tab_r.at[me], d).start()
    tab_r[me] = tab_s[me]

    for copy in small[:3]:
        copy.wait()
    sn_v[...] = nt(q_v[...].reshape(reqs * rows, HD), nk_v[...]).reshape(reqs, rows, HD)
    t_row = iota(t_v.shape, 0)
    t_col = iota(t_v.shape, 1)
    t_v[...] = jnp.where(
        t_row == (t_col // 128) * 16 + t_col % 16, 1.0, 0.0
    ).astype(BF16)
    hl_c[...] = jnp.zeros(hl_c.shape, F32)
    pl_c[...] = jnp.zeros(pl_c.shape, F32)
    lane = iota((rows, 128), 1)
    row = iota((rows, 128), 0)

    def home_part(c, between):
        home[c][0].wait()
        total = hl_c[0:rows]
        sums = []
        for j in range(per_chunk):
            r = c * per_chunk + j
            low = r * (2 * steps) + (row // (rows // 2)) * steps
            seen = (lane >= low) & (lane <= low + row % steps)
            new_scores = jnp.where(seen, sn_v[r], MASKED)
            scores = nt(wide_query(q_v[r]), hk_v[r])
            scores = jnp.where(iota(scores.shape, 1) < hlen[r], scores, MASKED)
            top = jnp.maximum(
                jnp.max(scores, axis=1, keepdims=True),
                jnp.max(new_scores, axis=1, keepdims=True),
            )
            shares = jnp.exp2((scores - top) * COEF)
            new_shares = jnp.exp2((new_scores - top) * COEF)
            summed = jnp.sum(shares, axis=1, keepdims=True) + jnp.sum(
                new_shares, axis=1, keepdims=True
            )
            hs_v[j] = shares.astype(BF16)
            hn_v[j] = new_shares.astype(BF16)
            sums.append(summed)
            total = jnp.where(lane == r, top * COEF + jnp.log2(summed), total)
            between(j)
        hl_c[0:rows] = total
        home[c][1].wait()
        for j in range(per_chunk):
            r = c * per_chunk + j
            both = nn(hs_v[j], hv_v[r])
            out = jnp.concatenate([both[:part_rows, :HD], both[part_rows:, HD:]], axis=0)
            out = out + nn(hn_v[j], nv_v[...])
            ho_v[r] = (out / sums[j]).astype(BF16)

    def nothing(j):
        pass

    home_part(0, nothing)
    home_part(1, nothing)

    all_of(0, tab_r).wait_recv()

    picks = {d: jnp.maximum(tab_r[pool_peer(d), 0, 0], 0) for d in FAR_FIRST}
    mine = jnp.maximum(tab_r[me, 0, 0], 0)
    halves = [slice(0, part_rows), slice(part_rows, rows)]

    def send_query(k, d):
        peer = pool_peer(d)
        qs[k][peer] = q_v[picks[d], halves[k]]
        remote(1 + k, qs[k].at[peer], qr[k].at[me], d).start()

    for k in range(2):
        qr[k][me] = q_v[mine, halves[k]]
    for d in FAR_FIRST:
        send_query(0, d)
    for copy in weights:
        copy.start()

    def query_sends(j):
        for d in FAR_FIRST[j * 8 : j * 8 + 8]:
            send_query(1, d)

    home_part(2, query_sends)
    home_part(3, nothing)
    for d in range(n):
        inv_s[d] = inv_v[pool_peer(d), 0, 0]

    small[3].wait()
    small[4].wait()
    part_lane = iota((part_rows, 128), 1)

    def send_result(k, d):
        peer = pool_peer(d)
        rs[k][peer] = res_v[inv_s[d], halves[k]]
        remote(4 + k, rs[k].at[peer], rr[k].at[me], d).start()

    def send_lse(d):
        remote(3, ls_v.at[pool_peer(d)], lr_v.at[me], d).start()

    for k in range(2):
        all_of(1 + k, qr[k]).wait_recv()
        width = slice(k * HD, k * HD + HD)
        total = jnp.zeros((part_rows, 128), F32)
        sums = []
        for l in range(slots):
            owner = lreq[l] // reqs
            shares, summed, lse = head_shares(qr[k][owner], pk_v[l, :, width], lblk[l] * BLOCK)
            sh_v[l] = shares
            sums.append(summed)
            total = jnp.where(part_lane == owner, lse, total)
        pl_c[halves[k]] = total
        if k == 1:
            ls_v[...] = pl_c[...].T[0:n].reshape(n, 1, 128)
            lr_v[me] = ls_v[me]
        for l in range(slots):
            out = nn(sh_v[l], pv_v[l, :, width])
            res_v[l, halves[k]] = (out / sums[l]).astype(BF16)
            if k == 1:
                for d in FAR_FIRST[2 * l : 2 * l + 2]:
                    send_lse(d)
        rr[k][me] = res_v[inv_s[0], halves[k]]
        if k == 0:
            for d in FAR_FIRST:
                send_result(0, d)
    eight = iota((8, 128), 1) // 16 == iota((8, 128), 0)
    local = tab_r[...].reshape(n, 128)
    parts = n + reqs
    seg = jnp.concatenate([local, iota((reqs, 128), 0)], axis=0)
    seg_lane = jnp.concatenate(
        [
            jnp.sum(jnp.where(eight, seg[c * 8 : c * 8 + 8], 0), axis=0, keepdims=True)
            for c in range(parts // 8)
        ],
        axis=1,
    )
    block = (16, parts * 16)
    b_row, b_col = iota(block, 0), iota(block, 1)
    head_step = b_col % 16 - b_row % steps
    owner_row = seg_lane - b_row // steps
    for i in range(16):
        same = (head_step == i // 4 * steps) & (owner_row == i % 4 * 4)
        e_v[i] = jnp.where(same, 1.0, 0.0).astype(BF16)
        for d in FAR_FIRST[2 * i : 2 * i + 2]:
            send_result(1, d)
    all_of(3, lr_v).wait_recv()
    lse = jnp.concatenate([lr_v[...].reshape(n, 128), hl_c[...].T[0:reqs]], axis=0)
    big = lse
    for r in range(reqs):
        hit = seg == r
        big = jnp.where(hit, jnp.max(jnp.where(hit, lse, MASKED), axis=0, keepdims=True), big)
    share = jnp.where(seg >= 0, jnp.exp2(lse - big), 0.0)
    total = jnp.ones_like(share)
    for r in range(reqs):
        hit = seg == r
        total = jnp.where(
            hit, jnp.sum(jnp.where(hit, share, 0.0), axis=0, keepdims=True), total
        )
    spread = nn((share / total).astype(BF16), t_v[...])

    def build(g):
        wide = g * 128
        along = jnp.concatenate(
            [
                jnp.sum(
                    jnp.where(eight, spread[c * 8 : c * 8 + 8, wide : wide + 128], 0.0),
                    axis=0,
                    keepdims=True,
                )
                for c in range(parts // 8)
            ],
            axis=1,
        )
        along = jnp.broadcast_to(along, block).astype(BF16)
        return (e_v[...] * along[None]).reshape(256, parts * 16)

    def merge(k, a_v, lefts):
        all_of(4 + k, rr[k]).wait_recv()
        for g in range(part_rows // 16):
            group = slice(g * 16, g * 16 + 16)
            own = slice(k * part_rows + g * 16, k * part_rows + g * 16 + 16)
            right = jnp.concatenate(
                [rr[k][:, group].reshape(n * 16, HD), ho_v[:, own].reshape(reqs * 16, HD)],
                axis=0,
            )
            merged = nn(lefts(g), right).astype(BF16)
            for h in range(4):
                head = g * 4 + h
                a_v[:, head * HD : head * HD + HD] = merged[h * rows : h * rows + rows]

    for g in range(2):
        l_v[g] = build(2 + g)
    merge(0, a0_v, build)
    for i in range(t):
        weights[i].wait()
        acc_v[i] = nn(a0_v[...], w_v[i, 0:deep])
    merge(1, a1_v, lambda g: l_v[g])

    half = cols // 2
    left, right = slice(0, half), slice(half, cols)

    def projected(i, at):
        return acc_v[i, :, at] + nn(a1_v[...], w_v[i, deep : 2 * deep, at])

    def to_neighbour(i, src, side):
        return pltpu.make_async_remote_copy(
            src_ref=src,
            dst_ref=pr_v.at[i],
            send_sem=rsend_sem.at[i],
            recv_sem=rrecv_sem.at[i],
            device_id={"tp": tp_peer(side), "pool": me},
            device_id_type=MESH,
        )

    up, down = 1, t - 1
    ring = [
        to_neighbour(i, ps_v.at[i], side)
        for i, side in enumerate([up, down, up, down, up, down])
    ]
    def send(i, value):
        ps_v[i] = value.astype(BF16)
        ring[i].start()

    send(0, projected(0, left))
    send(1, projected(0, right))
    send(2, projected(1, right))
    send(3, projected(2, left))
    above = projected(1, left)
    ring[0].wait_recv()
    send(4, above + pr_v[0].astype(F32))
    below = projected(2, right)
    ring[1].wait_recv()
    send(5, below + pr_v[1].astype(F32))
    own = jnp.concatenate([projected(3, left), projected(3, right)], axis=1)
    for i in range(2, 6):
        ring[i].wait_recv()
    from_below = jnp.concatenate([pr_v[4], pr_v[2]], axis=1).astype(F32)
    from_above = jnp.concatenate([pr_v[3], pr_v[5]], axis=1).astype(F32)
    result = own + from_below + from_above

    first = iota((8, 8, HD), 1) < 4
    for g in range(2):
        even, odd = [], []
        for k in range(2):
            c = (g * 2 + k) * 2 * HD
            left = result[:, c : c + HD].reshape(8, 8, HD)
            right = result[:, c + HD : c + 2 * HD].reshape(8, 8, HD)
            even.append(jnp.where(first, left, pltpu.roll(right, 4, 1)))
            odd.append(jnp.where(first, pltpu.roll(left, 4, 1), right))
        for k, both in enumerate([even, odd]):
            out_ref[:, k, g * 16 : g * 16 + 16] = jnp.concatenate(both, axis=1).astype(BF16)

    all_of(0, tab_s).wait_send()
    for k in range(2):
        all_of(1 + k, qs[k]).wait_send()
        all_of(4 + k, rs[k]).wait_send()
    all_of(3, ls_v).wait_send()
    for copy in ring:
        copy.wait_send()


def per_device(
    queries, home_keys, home_values, new_keys, new_values, home_len,
    piece_keys, piece_values, lend_request, lend_blocks, out_weight,
):
    n = lax.axis_size("pool")
    t = lax.axis_size("tp")
    reqs, steps, features = queries.shape
    heads = features // HD
    kv = new_keys.shape[2] // HD
    rows = heads * steps
    slots, piece = piece_keys.shape[:2]
    cols = out_weight.shape[1] // t

    def head_rows(x):
        count = x.shape[2] // HD
        return x.reshape(reqs, steps, count, HD).transpose(0, 2, 1, 3)

    q = head_rows(queries).reshape(reqs, rows, HD)
    nk = head_rows(new_keys).reshape(reqs * kv * steps, HD)
    nv = head_rows(new_values).reshape(reqs * kv * steps, HD)
    hbm = pl.BlockSpec(memory_space=pl.ANY)
    chunks = 4
    vmem = pltpu.VMEM
    out = pl.pallas_call(
        functools.partial(kernel, n, t),
        out_shape=vmem((reqs // 2, 2, cols // HD * steps, HD), BF16),
        in_specs=[hbm] * 11,
        out_specs=pl.BlockSpec(memory_space=pltpu.VMEM),
        scratch_shapes=[
            *[pltpu.SMEM((reqs,), jnp.int32)] * 3,
            vmem(q.shape, BF16),
            vmem(nk.shape, BF16),
            vmem(nv.shape, BF16),
            vmem(home_keys.shape, BF16),
            vmem(home_values.shape, BF16),
            vmem(piece_keys.shape, BF16),
            vmem(piece_values.shape, BF16),
            vmem((t, features, cols), BF16),
            vmem((reqs, rows, 128), F32),
            vmem((n, 1, 128), jnp.int32),
            vmem((n, 1, 128), jnp.int32),
            vmem((n, 1, 128), jnp.int32),
            pltpu.SMEM((n,), jnp.int32),
            *[vmem((n, rows // 2, HD), BF16)] * 4,
            vmem((slots, rows, HD), BF16),
            vmem((slots, rows // 2, piece), BF16),
            *[vmem((n, rows // 2, HD), BF16)] * 4,
            *[vmem((n, 1, 128), F32)] * 2,
            vmem((reqs, rows, HD), BF16),
            vmem((reqs // chunks, rows, home_keys.shape[1]), BF16),
            vmem((reqs // chunks, rows, 128), BF16),
            *[vmem((128, 128), F32)] * 2,
            vmem((16, 16, (n + reqs) * 16), BF16),
            vmem((128, (rows // 16) * 128), BF16),
            vmem((2, 256, (n + reqs) * 16), BF16),
            *[vmem((reqs * steps, features // 2), BF16)] * 2,
            vmem((t, reqs * steps, cols), F32),
            vmem((6, reqs * steps, cols // 2), BF16),
            vmem((6, reqs * steps, cols // 2), BF16),
            pltpu.SemaphoreType.DMA((8,)),
            pltpu.SemaphoreType.DMA((2, chunks)),
            pltpu.SemaphoreType.DMA((t,)),
            pltpu.SemaphoreType.DMA((6,)),
            pltpu.SemaphoreType.DMA((6,)),
            pltpu.SemaphoreType.DMA((6,)),
            pltpu.SemaphoreType.DMA((6,)),
        ],
        compiler_params=pltpu.CompilerParams(
            collective_id=0, has_side_effects=True, vmem_limit_bytes=56 * 1024 * 1024
        ),
        name="lent_attention",
    )(
        home_len, lend_request, lend_blocks, q, nk, nv,
        home_keys, home_values, piece_keys, piece_values, out_weight,
    )
    out = out.reshape(reqs, cols // HD, steps, HD).transpose(0, 2, 1, 3)
    return out.reshape(reqs, steps, cols)


def solution(mesh):
    placed = (
        P("pool", None, "tp"),
        P("pool", None, "tp"),
        P("pool", None, "tp"),
        P("pool", None, "tp"),
        P("pool", None, "tp"),
        P("pool"),
        P("pool", None, "tp"),
        P("pool", None, "tp"),
        P("pool"),
        P("pool"),
        P("tp", None),
    )
    return jax.shard_map(
        per_device, mesh=mesh, in_specs=placed, out_specs=P("pool", None, "tp"), check_vma=False
    )
```

```python
import functools
import math

import jax
import jax.numpy as jnp
from jax import lax
from jax.experimental import pallas as pl
from jax.experimental.pallas import tpu as pltpu
from jax.sharding import PartitionSpec as P

QH = 64
KVH = 8
HD = 128
BLOCK = 128
MASKED = -1e30
MESH = pl.DeviceIdType.MESH
F32 = jnp.float32
BF16 = jnp.bfloat16
COEF = math.log2(math.e) / math.sqrt(HD)


ORDER = list(range(1, 32))


def nt(a, b):
    return lax.dot_general(a, b, (((1,), (1,)), ((), ())), preferred_element_type=F32)


def nn(a, b):
    return lax.dot_general(a, b, (((1,), (0,)), ((), ())), preferred_element_type=F32)


def iota(shape, dim):
    return lax.broadcasted_iota(jnp.int32, shape, dim)


def wide_query(q):
    half = q.shape[0] // 2
    zero = jnp.zeros((half, HD), BF16)
    return jnp.concatenate(
        [
            jnp.concatenate([q[:half], zero], axis=1),
            jnp.concatenate([zero, q[half:]], axis=1),
        ],
        axis=0,
    )


def head_shares(q, keys, valid_len):
    scores = nt(q, keys)
    scores = jnp.where(iota(scores.shape, 1) < valid_len, scores, MASKED)
    top = jnp.max(scores, axis=1, keepdims=True)
    shares = jnp.exp2((scores - top) * COEF)
    summed = jnp.sum(shares, axis=1, keepdims=True)
    return shares.astype(BF16), summed, top * COEF + jnp.log2(summed)


def kernel(
    n, t,
    hlen_h, lreq_h, lblk_h, q_h, nk_h, nv_h, hk_h, hv_h, pk_h, pv_h, w_h,
    out_ref,
    hlen, lreq, lblk, q_v, nk_v, nv_v, hk_v, hv_v, pk_v, pv_v, w_v,
    sn_v, tab_s, tab_r, inv_v, inv_s,
    qs0_v, qs1_v, qr0_v, qr1_v, res_v, sh_v, rs0_v, rs1_v, rr0_v, rr1_v, ls_v, lr_v,
    ho_v, hs_v, hn_v, hl_c, pl_c, e_v, t_v, l_v, a0_v, a1_v, acc_v, ps_v, pr_v,
    in_sem, home_sem, w_sem, send_sem, recv_sem, rsend_sem, rrecv_sem,
):
    me = lax.axis_index("pool")
    tp = lax.axis_index("tp")
    reqs, rows, _ = q_v.shape
    slots = pk_v.shape[0]
    steps = 4
    home_chunks = home_sem.shape[1]
    per_chunk = reqs // home_chunks
    cols = w_v.shape[2]
    part_rows = rows // 2
    deep = a0_v.shape[1]
    qs, qr = (qs0_v, qs1_v), (qr0_v, qr1_v)
    rs, rr = (rs0_v, rs1_v), (rr0_v, rr1_v)

    core = lax.rem(me, 2)
    turn = 1 - 2 * core
    ys = [lax.rem(me // 8 + turn * d + 4, 4) for d in range(4)]
    xs = [lax.rem(me // 2 % 4 + turn * d + 4, 4) for d in range(4)]
    peers = {
        k: (ys[k % 4] * 4 + xs[(k // 4 + k) % 4]) * 2 + (core if k < 16 else 1 - core)
        for k in range(n)
    }

    def pool_peer(d):
        return peers[d]

    def tp_peer(d):
        return lax.rem(tp + d, t)

    barrier = pltpu.get_barrier_semaphore()

    for d in range(1, t):
        pl.semaphore_signal(
            barrier, inc=1, device_id={"tp": tp_peer(d), "pool": me}, device_id_type=MESH
        )
    for d in ORDER:
        pl.semaphore_signal(
            barrier, inc=1, device_id={"tp": tp, "pool": pool_peer(d)}, device_id_type=MESH
        )

    small = [
        pltpu.make_async_copy(src, dst, in_sem.at[i])
        for i, (src, dst) in enumerate(
            [
                (q_h, q_v), (nk_h, nk_v), (nv_h, nv_v), (pk_h, pk_v), (pv_h, pv_v),
                (lreq_h, lreq), (hlen_h, hlen), (lblk_h, lblk),
            ]
        )
    ]
    for i in (5, 6, 7, 0, 1, 2):
        small[i].start()
    home = []
    for c in range(home_chunks):
        part = pl.ds(c * per_chunk, per_chunk)
        home.append(
            [
                pltpu.make_async_copy(hk_h.at[part], hk_v.at[part], home_sem.at[0, c]),
                pltpu.make_async_copy(hv_h.at[part], hv_v.at[part], home_sem.at[1, c]),
            ]
        )
    for c in range(home_chunks):
        home[c][0].start()
        home[c][1].start()
    small[3].start()
    small[4].start()
    order = [2, 1, 3, 0]
    weights = []
    for i, d in enumerate(order):
        column = pl.multiple_of(tp_peer(d) * cols, cols)
        weights.append(
            pltpu.make_async_copy(w_h.at[:, pl.ds(column, cols)], w_v.at[i], w_sem.at[i])
        )

    for i in (5, 6, 7):
        small[i].wait()
    owner_id = iota((n, 128), 0)
    wanted = jnp.full((n, 128), -1, jnp.int32)
    slot_of = jnp.zeros((n, 128), jnp.int32)
    for l in range(slots):
        request = lreq[l]
        owner = request // reqs
        hit = owner_id == owner
        wanted = jnp.where(hit, request - owner * reqs, wanted)
        slot_of = jnp.where(hit, l, slot_of)
    tab_s[...] = wanted.reshape(n, 1, 128)
    inv_v[...] = slot_of.reshape(n, 1, 128)

    def remote(phase, src, dst, d):
        return pltpu.make_async_remote_copy(
            src_ref=src,
            dst_ref=dst,
            send_sem=send_sem.at[phase],
            recv_sem=recv_sem.at[phase],
            device_id={"tp": tp, "pool": pool_peer(d)},
            device_id_type=MESH,
        )

    def all_of(phase, buffer):
        part = buffer.at[pl.ds(0, n - 1)]
        return remote(phase, part, part, 1)

    pl.semaphore_wait(barrier, n - 1 + t - 1)

    for d in ORDER:
        remote(0, tab_s.at[pool_peer(d)], tab_r.at[me], d).start()
    tab_r[me] = tab_s[me]

    for copy in small[:3]:
        copy.wait()
    sn_v[...] = nt(q_v[...].reshape(reqs * rows, HD), nk_v[...]).reshape(reqs, rows, HD)
    t_row = iota(t_v.shape, 0)
    t_col = iota(t_v.shape, 1)
    t_v[...] = jnp.where(
        t_row == (t_col // 128) * 16 + t_col % 16, 1.0, 0.0
    ).astype(BF16)
    hl_c[...] = jnp.zeros(hl_c.shape, F32)
    pl_c[...] = jnp.zeros(pl_c.shape, F32)
    lane = iota((rows, 128), 1)
    row = iota((rows, 128), 0)

    def home_part(c, between):
        home[c][0].wait()
        total = hl_c[0:rows]
        sums = []
        for j in range(per_chunk):
            r = c * per_chunk + j
            low = r * (2 * steps) + (row // (rows // 2)) * steps
            seen = (lane >= low) & (lane <= low + row % steps)
            new_scores = jnp.where(seen, sn_v[r], MASKED)
            scores = nt(wide_query(q_v[r]), hk_v[r])
            scores = jnp.where(iota(scores.shape, 1) < hlen[r], scores, MASKED)
            top = jnp.maximum(
                jnp.max(scores, axis=1, keepdims=True),
                jnp.max(new_scores, axis=1, keepdims=True),
            )
            shares = jnp.exp2((scores - top) * COEF)
            new_shares = jnp.exp2((new_scores - top) * COEF)
            summed = jnp.sum(shares, axis=1, keepdims=True) + jnp.sum(
                new_shares, axis=1, keepdims=True
            )
            hs_v[j] = shares.astype(BF16)
            hn_v[j] = new_shares.astype(BF16)
            sums.append(summed)
            total = jnp.where(lane == r, top * COEF + jnp.log2(summed), total)
            between(j)
        hl_c[0:rows] = total
        home[c][1].wait()
        for j in range(per_chunk):
            r = c * per_chunk + j
            both = nn(hs_v[j], hv_v[r])
            out = jnp.concatenate([both[:part_rows, :HD], both[part_rows:, HD:]], axis=0)
            out = out + nn(hn_v[j], nv_v[...])
            ho_v[r] = (out / sums[j]).astype(BF16)

    def nothing(j):
        pass

    home_part(0, nothing)
    home_part(1, nothing)

    all_of(0, tab_r).wait_recv()

    picks = {d: jnp.maximum(tab_r[pool_peer(d), 0, 0], 0) for d in ORDER}
    mine = jnp.maximum(tab_r[me, 0, 0], 0)
    halves = [slice(0, part_rows), slice(part_rows, rows)]

    def send_query(k, d):
        peer = pool_peer(d)
        qs[k][peer] = q_v[picks[d], halves[k]]
        remote(1 + k, qs[k].at[peer], qr[k].at[me], d).start()

    for k in range(2):
        qr[k][me] = q_v[mine, halves[k]]
    for d in ORDER:
        send_query(0, d)
    for copy in weights:
        copy.start()

    def query_sends(j):
        for d in ORDER[j * 8 : j * 8 + 8]:
            send_query(1, d)

    home_part(2, query_sends)
    home_part(3, nothing)
    for d in range(n):
        inv_s[d] = inv_v[pool_peer(d), 0, 0]

    small[3].wait()
    small[4].wait()
    part_lane = iota((part_rows, 128), 1)

    def send_result(k, d):
        peer = pool_peer(d)
        rs[k][peer] = res_v[inv_s[d], halves[k]]
        remote(4 + k, rs[k].at[peer], rr[k].at[me], d).start()

    def send_lse(d):
        remote(3, ls_v.at[pool_peer(d)], lr_v.at[me], d).start()

    for k in range(2):
        all_of(1 + k, qr[k]).wait_recv()
        width = slice(k * HD, k * HD + HD)
        total = jnp.zeros((part_rows, 128), F32)
        sums = []
        for l in range(slots):
            owner = lreq[l] // reqs
            shares, summed, lse = head_shares(qr[k][owner], pk_v[l, :, width], lblk[l] * BLOCK)
            sh_v[l] = shares
            sums.append(summed)
            total = jnp.where(part_lane == owner, lse, total)
        pl_c[halves[k]] = total
        if k == 1:
            ls_v[...] = pl_c[...].T[0:n].reshape(n, 1, 128)
            lr_v[me] = ls_v[me]
        for l in range(slots):
            out = nn(sh_v[l], pv_v[l, :, width])
            res_v[l, halves[k]] = (out / sums[l]).astype(BF16)
            if k == 1:
                for d in ORDER[2 * l : 2 * l + 2]:
                    send_lse(d)
        rr[k][me] = res_v[inv_s[0], halves[k]]
        if k == 0:
            for d in ORDER:
                send_result(0, d)
    eight = iota((8, 128), 1) // 16 == iota((8, 128), 0)
    local = tab_r[...].reshape(n, 128)
    parts = n + reqs
    seg = jnp.concatenate([local, iota((reqs, 128), 0)], axis=0)
    seg_lane = jnp.concatenate(
        [
            jnp.sum(jnp.where(eight, seg[c * 8 : c * 8 + 8], 0), axis=0, keepdims=True)
            for c in range(parts // 8)
        ],
        axis=1,
    )
    block = (16, parts * 16)
    b_row, b_col = iota(block, 0), iota(block, 1)
    head_step = b_col % 16 - b_row % steps
    owner_row = seg_lane - b_row // steps
    for i in range(16):
        same = (head_step == i // 4 * steps) & (owner_row == i % 4 * 4)
        e_v[i] = jnp.where(same, 1.0, 0.0).astype(BF16)
        for d in ORDER[2 * i : 2 * i + 2]:
            send_result(1, d)
    all_of(3, lr_v).wait_recv()
    lse = jnp.concatenate([lr_v[...].reshape(n, 128), hl_c[...].T[0:reqs]], axis=0)
    big = lse
    for r in range(reqs):
        hit = seg == r
        big = jnp.where(hit, jnp.max(jnp.where(hit, lse, MASKED), axis=0, keepdims=True), big)
    share = jnp.where(seg >= 0, jnp.exp2(lse - big), 0.0)
    total = jnp.ones_like(share)
    for r in range(reqs):
        hit = seg == r
        total = jnp.where(
            hit, jnp.sum(jnp.where(hit, share, 0.0), axis=0, keepdims=True), total
        )
    spread = nn((share / total).astype(BF16), t_v[...])

    def build(g):
        wide = g * 128
        along = jnp.concatenate(
            [
                jnp.sum(
                    jnp.where(eight, spread[c * 8 : c * 8 + 8, wide : wide + 128], 0.0),
                    axis=0,
                    keepdims=True,
                )
                for c in range(parts // 8)
            ],
            axis=1,
        )
        along = jnp.broadcast_to(along, block).astype(BF16)
        return (e_v[...] * along[None]).reshape(256, parts * 16)

    def merge(k, a_v, lefts):
        all_of(4 + k, rr[k]).wait_recv()
        for g in range(part_rows // 16):
            group = slice(g * 16, g * 16 + 16)
            own = slice(k * part_rows + g * 16, k * part_rows + g * 16 + 16)
            right = jnp.concatenate(
                [rr[k][:, group].reshape(n * 16, HD), ho_v[:, own].reshape(reqs * 16, HD)],
                axis=0,
            )
            merged = nn(lefts(g), right).astype(BF16)
            for h in range(4):
                head = g * 4 + h
                a_v[:, head * HD : head * HD + HD] = merged[h * rows : h * rows + rows]

    for g in range(2):
        l_v[g] = build(2 + g)
    merge(0, a0_v, build)
    for i in range(t):
        weights[i].wait()
        acc_v[i] = nn(a0_v[...], w_v[i, 0:deep])
    merge(1, a1_v, lambda g: l_v[g])

    half = cols // 2
    left, right = slice(0, half), slice(half, cols)

    def projected(i, at):
        return acc_v[i, :, at] + nn(a1_v[...], w_v[i, deep : 2 * deep, at])

    def to_neighbour(i, src, side):
        return pltpu.make_async_remote_copy(
            src_ref=src,
            dst_ref=pr_v.at[i],
            send_sem=rsend_sem.at[i],
            recv_sem=rrecv_sem.at[i],
            device_id={"tp": tp_peer(side), "pool": me},
            device_id_type=MESH,
        )

    up, down = 1, t - 1
    ring = [
        to_neighbour(i, ps_v.at[i], side)
        for i, side in enumerate([up, down, up, down, up, down])
    ]
    def send(i, value):
        ps_v[i] = value.astype(BF16)
        ring[i].start()

    send(0, projected(0, left))
    send(1, projected(0, right))
    send(2, projected(1, right))
    send(3, projected(2, left))
    above = projected(1, left)
    ring[0].wait_recv()
    send(4, above + pr_v[0].astype(F32))
    below = projected(2, right)
    ring[1].wait_recv()
    send(5, below + pr_v[1].astype(F32))
    own = jnp.concatenate([projected(3, left), projected(3, right)], axis=1)
    for i in range(2, 6):
        ring[i].wait_recv()
    from_below = jnp.concatenate([pr_v[4], pr_v[2]], axis=1).astype(F32)
    from_above = jnp.concatenate([pr_v[3], pr_v[5]], axis=1).astype(F32)
    result = own + from_below + from_above

    first = iota((8, 8, HD), 1) < 4
    for g in range(2):
        even, odd = [], []
        for k in range(2):
            c = (g * 2 + k) * 2 * HD
            left = result[:, c : c + HD].reshape(8, 8, HD)
            right = result[:, c + HD : c + 2 * HD].reshape(8, 8, HD)
            even.append(jnp.where(first, left, pltpu.roll(right, 4, 1)))
            odd.append(jnp.where(first, pltpu.roll(left, 4, 1), right))
        for k, both in enumerate([even, odd]):
            out_ref[:, k, g * 16 : g * 16 + 16] = jnp.concatenate(both, axis=1).astype(BF16)

    all_of(0, tab_s).wait_send()
    for k in range(2):
        all_of(1 + k, qs[k]).wait_send()
        all_of(4 + k, rs[k]).wait_send()
    all_of(3, ls_v).wait_send()
    for copy in ring:
        copy.wait_send()


def per_device(
    queries, home_keys, home_values, new_keys, new_values, home_len,
    piece_keys, piece_values, lend_request, lend_blocks, out_weight,
):
    n = lax.axis_size("pool")
    t = lax.axis_size("tp")
    reqs, steps, features = queries.shape
    heads = features // HD
    kv = new_keys.shape[2] // HD
    rows = heads * steps
    slots, piece = piece_keys.shape[:2]
    cols = out_weight.shape[1] // t

    def head_rows(x):
        count = x.shape[2] // HD
        return x.reshape(reqs, steps, count, HD).transpose(0, 2, 1, 3)

    q = head_rows(queries).reshape(reqs, rows, HD)
    nk = head_rows(new_keys).reshape(reqs * kv * steps, HD)
    nv = head_rows(new_values).reshape(reqs * kv * steps, HD)
    hbm = pl.BlockSpec(memory_space=pl.ANY)
    chunks = 4
    vmem = pltpu.VMEM
    out = pl.pallas_call(
        functools.partial(kernel, n, t),
        out_shape=vmem((reqs // 2, 2, cols // HD * steps, HD), BF16),
        in_specs=[hbm] * 11,
        out_specs=pl.BlockSpec(memory_space=pltpu.VMEM),
        scratch_shapes=[
            *[pltpu.SMEM((reqs,), jnp.int32)] * 3,
            vmem(q.shape, BF16),
            vmem(nk.shape, BF16),
            vmem(nv.shape, BF16),
            vmem(home_keys.shape, BF16),
            vmem(home_values.shape, BF16),
            vmem(piece_keys.shape, BF16),
            vmem(piece_values.shape, BF16),
            vmem((t, features, cols), BF16),
            vmem((reqs, rows, 128), F32),
            vmem((n, 1, 128), jnp.int32),
            vmem((n, 1, 128), jnp.int32),
            vmem((n, 1, 128), jnp.int32),
            pltpu.SMEM((n,), jnp.int32),
            *[vmem((n, rows // 2, HD), BF16)] * 4,
            vmem((slots, rows, HD), BF16),
            vmem((slots, rows // 2, piece), BF16),
            *[vmem((n, rows // 2, HD), BF16)] * 4,
            *[vmem((n, 1, 128), F32)] * 2,
            vmem((reqs, rows, HD), BF16),
            vmem((reqs // chunks, rows, home_keys.shape[1]), BF16),
            vmem((reqs // chunks, rows, 128), BF16),
            *[vmem((128, 128), F32)] * 2,
            vmem((16, 16, (n + reqs) * 16), BF16),
            vmem((128, (rows // 16) * 128), BF16),
            vmem((2, 256, (n + reqs) * 16), BF16),
            *[vmem((reqs * steps, features // 2), BF16)] * 2,
            vmem((t, reqs * steps, cols), F32),
            vmem((6, reqs * steps, cols // 2), BF16),
            vmem((6, reqs * steps, cols // 2), BF16),
            pltpu.SemaphoreType.DMA((8,)),
            pltpu.SemaphoreType.DMA((2, chunks)),
            pltpu.SemaphoreType.DMA((t,)),
            pltpu.SemaphoreType.DMA((6,)),
            pltpu.SemaphoreType.DMA((6,)),
            pltpu.SemaphoreType.DMA((6,)),
            pltpu.SemaphoreType.DMA((6,)),
        ],
        compiler_params=pltpu.CompilerParams(
            collective_id=0, has_side_effects=True, vmem_limit_bytes=56 * 1024 * 1024
        ),
        name="lent_attention",
    )(
        home_len, lend_request, lend_blocks, q, nk, nv,
        home_keys, home_values, piece_keys, piece_values, out_weight,
    )
    out = out.reshape(reqs, cols // HD, steps, HD).transpose(0, 2, 1, 3)
    return out.reshape(reqs, steps, cols)


def solution(mesh):
    placed = (
        P("pool", None, "tp"),
        P("pool", None, "tp"),
        P("pool", None, "tp"),
        P("pool", None, "tp"),
        P("pool", None, "tp"),
        P("pool"),
        P("pool", None, "tp"),
        P("pool", None, "tp"),
        P("pool"),
        P("pool"),
        P("tp", None),
    )
    return jax.shard_map(
        per_device, mesh=mesh, in_specs=placed, out_specs=P("pool", None, "tp"), check_vma=False
    )
```

```python
import functools
import math

import jax
import jax.numpy as jnp
from jax import lax
from jax.experimental import pallas as pl
from jax.experimental.pallas import tpu as pltpu
from jax.sharding import PartitionSpec as P

QH = 64
KVH = 8
HD = 128
BLOCK = 128
MASKED = -1e30
MESH = pl.DeviceIdType.MESH
F32 = jnp.float32
BF16 = jnp.bfloat16
COEF = math.log2(math.e) / math.sqrt(HD)


def hops(d):
    dy, dx = d // 8, d // 2 % 4
    return min(dy, 4 - dy) + min(dx, 4 - dx)


FAR_FIRST = sorted(range(1, 32), key=lambda d: -hops(d))


def nt(a, b):
    return lax.dot_general(a, b, (((1,), (1,)), ((), ())), preferred_element_type=F32)


def nn(a, b):
    return lax.dot_general(a, b, (((1,), (0,)), ((), ())), preferred_element_type=F32)


def iota(shape, dim):
    return lax.broadcasted_iota(jnp.int32, shape, dim)


def wide_query(q):
    half = q.shape[0] // 2
    zero = jnp.zeros((half, HD), BF16)
    return jnp.concatenate(
        [
            jnp.concatenate([q[:half], zero], axis=1),
            jnp.concatenate([zero, q[half:]], axis=1),
        ],
        axis=0,
    )


def head_shares(q, keys, valid_len):
    scores = nt(q, keys)
    scores = jnp.where(iota(scores.shape, 1) < valid_len, scores, MASKED)
    top = jnp.max(scores, axis=1, keepdims=True)
    shares = jnp.exp2((scores - top) * COEF)
    summed = jnp.sum(shares, axis=1, keepdims=True)
    return shares.astype(BF16), summed, top * COEF + jnp.log2(summed)


def kernel(
    n, t,
    hlen_h, lreq_h, lblk_h, q_h, nk_h, nv_h, hk_h, hv_h, pk_h, pv_h, w_h,
    out_ref,
    hlen, lreq, lblk, q_v, nk_v, nv_v, hk_v, hv_v, pk_v, pv_v, w_v,
    sn_v, tab_s, tab_r, inv_v, inv_s,
    qs_v, qr_v, res_v, sh_v, rs0_v, rs1_v, rr0_v, rr1_v, ls_v, lr_v,
    ho_v, hs_v, hn_v, hl_c, pl_c, e_v, t_v, l_v, a0_v, a1_v, acc_v, ps_v, pr_v,
    in_sem, home_sem, w_sem, send_sem, recv_sem, rsend_sem, rrecv_sem,
):
    me = lax.axis_index("pool")
    tp = lax.axis_index("tp")
    reqs, rows, _ = q_v.shape
    slots = pk_v.shape[0]
    steps = 4
    home_chunks = home_sem.shape[1]
    per_chunk = reqs // home_chunks
    cols = w_v.shape[2]
    part_rows = rows // 2
    deep = a0_v.shape[1]
    rs, rr = (rs0_v, rs1_v), (rr0_v, rr1_v)

    peers = {d: jnp.where(me + d >= n, me + d - n, me + d) for d in range(n)}

    def pool_peer(d):
        return peers[d]

    def tp_peer(d):
        return lax.rem(tp + d, t)

    barrier = pltpu.get_barrier_semaphore()

    for d in range(1, t):
        pl.semaphore_signal(
            barrier, inc=1, device_id={"tp": tp_peer(d), "pool": me}, device_id_type=MESH
        )
    for d in FAR_FIRST:
        pl.semaphore_signal(
            barrier, inc=1, device_id={"tp": tp, "pool": pool_peer(d)}, device_id_type=MESH
        )

    small = [
        pltpu.make_async_copy(src, dst, in_sem.at[i])
        for i, (src, dst) in enumerate(
            [
                (q_h, q_v), (nk_h, nk_v), (nv_h, nv_v), (pk_h, pk_v), (pv_h, pv_v),
                (lreq_h, lreq), (hlen_h, hlen), (lblk_h, lblk),
            ]
        )
    ]
    for i in (5, 6, 7, 0, 1, 2):
        small[i].start()
    home = []
    for c in range(home_chunks):
        part = pl.ds(c * per_chunk, per_chunk)
        home.append(
            [
                pltpu.make_async_copy(hk_h.at[part], hk_v.at[part], home_sem.at[0, c]),
                pltpu.make_async_copy(hv_h.at[part], hv_v.at[part], home_sem.at[1, c]),
            ]
        )
    for c in range(home_chunks):
        home[c][0].start()
        home[c][1].start()
    small[3].start()
    small[4].start()
    order = [2, 1, 3, 0]
    weights = []
    for i, d in enumerate(order):
        column = pl.multiple_of(tp_peer(d) * cols, cols)
        weights.append(
            pltpu.make_async_copy(w_h.at[:, pl.ds(column, cols)], w_v.at[i], w_sem.at[i])
        )

    for i in (5, 6, 7):
        small[i].wait()
    owner_id = iota((n, 128), 0)
    wanted = jnp.full((n, 128), -1, jnp.int32)
    slot_of = jnp.zeros((n, 128), jnp.int32)
    for l in range(slots):
        request = lreq[l]
        owner = request // reqs
        hit = owner_id == owner
        wanted = jnp.where(hit, request - owner * reqs, wanted)
        slot_of = jnp.where(hit, l, slot_of)
    tab_s[...] = wanted.reshape(n, 1, 128)
    inv_v[...] = slot_of.reshape(n, 1, 128)

    def remote(phase, src, dst, d):
        return pltpu.make_async_remote_copy(
            src_ref=src,
            dst_ref=dst,
            send_sem=send_sem.at[phase],
            recv_sem=recv_sem.at[phase],
            device_id={"tp": tp, "pool": pool_peer(d)},
            device_id_type=MESH,
        )

    def all_of(phase, buffer):
        part = buffer.at[pl.ds(0, n - 1)]
        return remote(phase, part, part, 1)

    pl.semaphore_wait(barrier, n - 1 + t - 1)

    for d in FAR_FIRST:
        remote(0, tab_s.at[pool_peer(d)], tab_r.at[me], d).start()
    tab_r[me] = tab_s[me]

    for copy in small[:3]:
        copy.wait()
    sn_v[...] = nt(q_v[...].reshape(reqs * rows, HD), nk_v[...]).reshape(reqs, rows, HD)
    t_row = iota(t_v.shape, 0)
    t_col = iota(t_v.shape, 1)
    t_v[...] = jnp.where(
        t_row == (t_col // 128) * 16 + t_col % 16, 1.0, 0.0
    ).astype(BF16)
    hl_c[...] = jnp.zeros(hl_c.shape, F32)
    pl_c[...] = jnp.zeros(pl_c.shape, F32)
    lane = iota((rows, 128), 1)
    row = iota((rows, 128), 0)

    def home_part(c, between):
        home[c][0].wait()
        total = hl_c[0:rows]
        sums = []
        for j in range(per_chunk):
            r = c * per_chunk + j
            low = r * (2 * steps) + (row // (rows // 2)) * steps
            seen = (lane >= low) & (lane <= low + row % steps)
            new_scores = jnp.where(seen, sn_v[r], MASKED)
            scores = nt(wide_query(q_v[r]), hk_v[r])
            scores = jnp.where(iota(scores.shape, 1) < hlen[r], scores, MASKED)
            top = jnp.maximum(
                jnp.max(scores, axis=1, keepdims=True),
                jnp.max(new_scores, axis=1, keepdims=True),
            )
            shares = jnp.exp2((scores - top) * COEF)
            new_shares = jnp.exp2((new_scores - top) * COEF)
            summed = jnp.sum(shares, axis=1, keepdims=True) + jnp.sum(
                new_shares, axis=1, keepdims=True
            )
            hs_v[j] = shares.astype(BF16)
            hn_v[j] = new_shares.astype(BF16)
            sums.append(summed)
            total = jnp.where(lane == r, top * COEF + jnp.log2(summed), total)
            between(j)
        hl_c[0:rows] = total
        home[c][1].wait()
        for j in range(per_chunk):
            r = c * per_chunk + j
            both = nn(hs_v[j], hv_v[r])
            out = jnp.concatenate([both[:part_rows, :HD], both[part_rows:, HD:]], axis=0)
            out = out + nn(hn_v[j], nv_v[...])
            ho_v[r] = (out / sums[j]).astype(BF16)

    def nothing(j):
        pass

    home_part(0, nothing)
    home_part(1, nothing)

    all_of(0, tab_r).wait_recv()

    picks = {d: jnp.maximum(tab_r[pool_peer(d), 0, 0], 0) for d in FAR_FIRST}
    mine = jnp.maximum(tab_r[me, 0, 0], 0)
    halves = [slice(0, part_rows), slice(part_rows, rows)]

    def send_query(d):
        peer = pool_peer(d)
        qs_v[peer] = q_v[picks[d]]
        remote(1, qs_v.at[peer], qr_v.at[me], d).start()

    qr_v[me] = q_v[mine]
    for d in FAR_FIRST:
        send_query(d)
    for copy in weights:
        copy.start()

    home_part(2, nothing)
    home_part(3, nothing)
    for d in range(n):
        inv_s[d] = inv_v[pool_peer(d), 0, 0]

    small[3].wait()
    small[4].wait()
    part_lane = iota((part_rows, 128), 1)

    def send_result(k, d):
        peer = pool_peer(d)
        rs[k][peer] = res_v[inv_s[d], halves[k]]
        remote(4 + k, rs[k].at[peer], rr[k].at[me], d).start()

    def send_lse(d):
        remote(3, ls_v.at[pool_peer(d)], lr_v.at[me], d).start()

    all_of(1, qr_v).wait_recv()
    for k in range(2):
        width = slice(k * HD, k * HD + HD)
        total = jnp.zeros((part_rows, 128), F32)
        sums = []
        for l in range(slots):
            owner = lreq[l] // reqs
            shares, summed, lse = head_shares(qr_v[owner, halves[k]], pk_v[l, :, width], lblk[l] * BLOCK)
            sh_v[l] = shares
            sums.append(summed)
            total = jnp.where(part_lane == owner, lse, total)
            if k == 1:
                for d in FAR_FIRST[2 * l : 2 * l + 2]:
                    send_result(0, d)
        pl_c[halves[k]] = total
        if k == 1:
            ls_v[...] = pl_c[...].T[0:n].reshape(n, 1, 128)
            lr_v[me] = ls_v[me]
        for l in range(slots):
            out = nn(sh_v[l], pv_v[l, :, width])
            res_v[l, halves[k]] = (out / sums[l]).astype(BF16)
            if k == 1:
                for d in FAR_FIRST[2 * l : 2 * l + 2]:
                    send_lse(d)
        rr[k][me] = res_v[inv_s[0], halves[k]]
    eight = iota((8, 128), 1) // 16 == iota((8, 128), 0)
    local = tab_r[...].reshape(n, 128)
    parts = n + reqs
    seg = jnp.concatenate([local, iota((reqs, 128), 0)], axis=0)
    seg_lane = jnp.concatenate(
        [
            jnp.sum(jnp.where(eight, seg[c * 8 : c * 8 + 8], 0), axis=0, keepdims=True)
            for c in range(parts // 8)
        ],
        axis=1,
    )
    block = (16, parts * 16)
    b_row, b_col = iota(block, 0), iota(block, 1)
    head_step = b_col % 16 - b_row % steps
    owner_row = seg_lane - b_row // steps
    for i in range(16):
        same = (head_step == i // 4 * steps) & (owner_row == i % 4 * 4)
        e_v[i] = jnp.where(same, 1.0, 0.0).astype(BF16)
        for d in FAR_FIRST[2 * i : 2 * i + 2]:
            send_result(1, d)
    all_of(3, lr_v).wait_recv()
    lse = jnp.concatenate([lr_v[...].reshape(n, 128), hl_c[...].T[0:reqs]], axis=0)
    big = lse
    for r in range(reqs):
        hit = seg == r
        big = jnp.where(hit, jnp.max(jnp.where(hit, lse, MASKED), axis=0, keepdims=True), big)
    share = jnp.where(seg >= 0, jnp.exp2(lse - big), 0.0)
    total = jnp.ones_like(share)
    for r in range(reqs):
        hit = seg == r
        total = jnp.where(
            hit, jnp.sum(jnp.where(hit, share, 0.0), axis=0, keepdims=True), total
        )
    spread = nn((share / total).astype(BF16), t_v[...])

    def build(g):
        wide = g * 128
        along = jnp.concatenate(
            [
                jnp.sum(
                    jnp.where(eight, spread[c * 8 : c * 8 + 8, wide : wide + 128], 0.0),
                    axis=0,
                    keepdims=True,
                )
                for c in range(parts // 8)
            ],
            axis=1,
        )
        along = jnp.broadcast_to(along, block).astype(BF16)
        return (e_v[...] * along[None]).reshape(256, parts * 16)

    def merge(k, a_v, lefts):
        all_of(4 + k, rr[k]).wait_recv()
        for g in range(part_rows // 16):
            group = slice(g * 16, g * 16 + 16)
            own = slice(k * part_rows + g * 16, k * part_rows + g * 16 + 16)
            right = jnp.concatenate(
                [rr[k][:, group].reshape(n * 16, HD), ho_v[:, own].reshape(reqs * 16, HD)],
                axis=0,
            )
            merged = nn(lefts(g), right).astype(BF16)
            for h in range(4):
                head = g * 4 + h
                a_v[:, head * HD : head * HD + HD] = merged[h * rows : h * rows + rows]

    for g in range(2):
        l_v[g] = build(2 + g)
    merge(0, a0_v, build)
    for i in range(t):
        weights[i].wait()
        acc_v[i] = nn(a0_v[...], w_v[i, 0:deep])
    merge(1, a1_v, lambda g: l_v[g])

    half = cols // 2
    left, right = slice(0, half), slice(half, cols)

    def projected(i, at):
        return acc_v[i, :, at] + nn(a1_v[...], w_v[i, deep : 2 * deep, at])

    def to_neighbour(i, src, side):
        return pltpu.make_async_remote_copy(
            src_ref=src,
            dst_ref=pr_v.at[i],
            send_sem=rsend_sem.at[i],
            recv_sem=rrecv_sem.at[i],
            device_id={"tp": tp_peer(side), "pool": me},
            device_id_type=MESH,
        )

    up, down = 1, t - 1
    ring = [
        to_neighbour(i, ps_v.at[i], side)
        for i, side in enumerate([up, down, up, down, up, down])
    ]
    def send(i, value):
        ps_v[i] = value.astype(BF16)
        ring[i].start()

    send(0, projected(0, left))
    send(1, projected(0, right))
    send(2, projected(1, right))
    send(3, projected(2, left))
    above = projected(1, left)
    ring[0].wait_recv()
    send(4, above + pr_v[0].astype(F32))
    below = projected(2, right)
    ring[1].wait_recv()
    send(5, below + pr_v[1].astype(F32))
    own = jnp.concatenate([projected(3, left), projected(3, right)], axis=1)
    for i in range(2, 6):
        ring[i].wait_recv()
    from_below = jnp.concatenate([pr_v[4], pr_v[2]], axis=1).astype(F32)
    from_above = jnp.concatenate([pr_v[3], pr_v[5]], axis=1).astype(F32)
    result = own + from_below + from_above

    first = iota((8, 8, HD), 1) < 4
    for g in range(2):
        even, odd = [], []
        for k in range(2):
            c = (g * 2 + k) * 2 * HD
            left = result[:, c : c + HD].reshape(8, 8, HD)
            right = result[:, c + HD : c + 2 * HD].reshape(8, 8, HD)
            even.append(jnp.where(first, left, pltpu.roll(right, 4, 1)))
            odd.append(jnp.where(first, pltpu.roll(left, 4, 1), right))
        for k, both in enumerate([even, odd]):
            out_ref[:, k, g * 16 : g * 16 + 16] = jnp.concatenate(both, axis=1).astype(BF16)

    all_of(0, tab_s).wait_send()
    for k in range(2):
        all_of(4 + k, rs[k]).wait_send()
    all_of(1, qs_v).wait_send()
    all_of(3, ls_v).wait_send()
    for copy in ring:
        copy.wait_send()


def per_device(
    queries, home_keys, home_values, new_keys, new_values, home_len,
    piece_keys, piece_values, lend_request, lend_blocks, out_weight,
):
    n = lax.axis_size("pool")
    t = lax.axis_size("tp")
    reqs, steps, features = queries.shape
    heads = features // HD
    kv = new_keys.shape[2] // HD
    rows = heads * steps
    slots, piece = piece_keys.shape[:2]
    cols = out_weight.shape[1] // t

    def head_rows(x):
        count = x.shape[2] // HD
        return x.reshape(reqs, steps, count, HD).transpose(0, 2, 1, 3)

    q = head_rows(queries).reshape(reqs, rows, HD)
    nk = head_rows(new_keys).reshape(reqs * kv * steps, HD)
    nv = head_rows(new_values).reshape(reqs * kv * steps, HD)
    hbm = pl.BlockSpec(memory_space=pl.ANY)
    chunks = 4
    vmem = pltpu.VMEM
    out = pl.pallas_call(
        functools.partial(kernel, n, t),
        out_shape=vmem((reqs // 2, 2, cols // HD * steps, HD), BF16),
        in_specs=[hbm] * 11,
        out_specs=pl.BlockSpec(memory_space=pltpu.VMEM),
        scratch_shapes=[
            *[pltpu.SMEM((reqs,), jnp.int32)] * 3,
            vmem(q.shape, BF16),
            vmem(nk.shape, BF16),
            vmem(nv.shape, BF16),
            vmem(home_keys.shape, BF16),
            vmem(home_values.shape, BF16),
            vmem(piece_keys.shape, BF16),
            vmem(piece_values.shape, BF16),
            vmem((t, features, cols), BF16),
            vmem((reqs, rows, 128), F32),
            vmem((n, 1, 128), jnp.int32),
            vmem((n, 1, 128), jnp.int32),
            vmem((n, 1, 128), jnp.int32),
            pltpu.SMEM((n,), jnp.int32),
            *[vmem((n, rows, HD), BF16)] * 2,
            vmem((slots, rows, HD), BF16),
            vmem((slots, rows // 2, piece), BF16),
            *[vmem((n, rows // 2, HD), BF16)] * 4,
            *[vmem((n, 1, 128), F32)] * 2,
            vmem((reqs, rows, HD), BF16),
            vmem((reqs // chunks, rows, home_keys.shape[1]), BF16),
            vmem((reqs // chunks, rows, 128), BF16),
            *[vmem((128, 128), F32)] * 2,
            vmem((16, 16, (n + reqs) * 16), BF16),
            vmem((128, (rows // 16) * 128), BF16),
            vmem((2, 256, (n + reqs) * 16), BF16),
            *[vmem((reqs * steps, features // 2), BF16)] * 2,
            vmem((t, reqs * steps, cols), F32),
            vmem((6, reqs * steps, cols // 2), BF16),
            vmem((6, reqs * steps, cols // 2), BF16),
            pltpu.SemaphoreType.DMA((8,)),
            pltpu.SemaphoreType.DMA((2, chunks)),
            pltpu.SemaphoreType.DMA((t,)),
            pltpu.SemaphoreType.DMA((6,)),
            pltpu.SemaphoreType.DMA((6,)),
            pltpu.SemaphoreType.DMA((6,)),
            pltpu.SemaphoreType.DMA((6,)),
        ],
        compiler_params=pltpu.CompilerParams(
            collective_id=0, has_side_effects=True, vmem_limit_bytes=56 * 1024 * 1024
        ),
        name="lent_attention",
    )(
        home_len, lend_request, lend_blocks, q, nk, nv,
        home_keys, home_values, piece_keys, piece_values, out_weight,
    )
    out = out.reshape(reqs, cols // HD, steps, HD).transpose(0, 2, 1, 3)
    return out.reshape(reqs, steps, cols)


def solution(mesh):
    placed = (
        P("pool", None, "tp"),
        P("pool", None, "tp"),
        P("pool", None, "tp"),
        P("pool", None, "tp"),
        P("pool", None, "tp"),
        P("pool"),
        P("pool", None, "tp"),
        P("pool", None, "tp"),
        P("pool"),
        P("pool"),
        P("tp", None),
    )
    return jax.shard_map(
        per_device, mesh=mesh, in_specs=placed, out_specs=P("pool", None, "tp"), check_vma=False
    )
```
